128 devices in a mesh: src: 8 (over x, y_lo), snk: 16 (over z, y_hi, core).
Axes of the slice: x: 4, y: 4 (y_hi: 2, y_lo: 2; y = y_hi * 2 + y_lo), z: 4, core: 2. Of those that a mesh axis runs over, the one named last changes fastest.
Arguments:
- elementals: bfloat16 [32, 8, 2, 256, 256], P('snk', 'src'), may hold values from -0.25 to 0.25
- perambulators: float32 [8, 32, 2, 256, 256], P('src', 'snk'), may hold values from -0.25 to 0.25
- source_times: int32 [8], replicated, may hold values from 0 to 31, as said below
- pair_index: int32 [8, 2], replicated, may hold values from 0 to 7, as said below
Outputs:
- boxes: float32 [2, 8, 8, 32], P(None, None, 'src', 'snk')
- crossed: float32 [2, 8, 8, 32], P(None, None, 'src', 'snk')
The draws below stay inside these ranges and needn't reach their ends.
Inputs may be any that keep to these rules, and one draw needn't show every extreme that they name: `source_times`: source times are distinct and always include the first and the last sink time. `pair_index`: each row names two different momenta, and every momentum is the first entry of exactly one row.
All inputs are finite; a program needn't handle non-finite values.
Results may differ from the reference program's by a relative error of at most 0.0088.
Values may be sent and summed in bfloat16 or wider, within the bound.
A program may use at most 128 MiB of HBM per device.

```python
import jax
import jax.numpy as jnp
from jax import lax

N = 256
MOM = 8
PAIRS = 8
NT = 32
NSRC = 8


def draw_source_times(key, part):
    key = jax.random.fold_in(key, 11)
    inner_key, order_key = jax.random.split(key)
    inner = jax.random.permutation(inner_key, NT - 2)[:NSRC - 2] + 1
    chosen = jnp.concatenate([jnp.array([0, NT - 1], dtype=jnp.int32), inner.astype(jnp.int32)])
    order = jax.random.permutation(order_key, NSRC)
    return chosen[order].astype(jnp.int32)


def draw_pair_index(key, part):
    key = jax.random.fold_in(key, 23)
    first_key, step_key = jax.random.split(key)
    first_mom = jax.random.permutation(first_key, MOM)[:PAIRS].astype(jnp.int32)
    stride = jax.random.randint(step_key, (PAIRS,), 1, MOM).astype(jnp.int32)
    second_mom = (first_mom + stride) % MOM
    return jnp.stack([first_mom, second_mom], axis=1).astype(jnp.int32)


def block_scale(key, extent, cuts, smallest, largest):
    factor_of = 1.0
    for dim, shards_of in cuts:
        heights = jax.random.uniform(jax.random.fold_in(jax.random.fold_in(key, 6), dim), (shards_of,), jnp.float32, smallest / len(cuts), largest / len(cuts))
        factor_of = factor_of * jnp.repeat(jnp.exp(heights), extent[dim] // shards_of).reshape((-1,) + (1,) * (len(extent) - 1 - dim))
    return factor_of


def centred(stream_key, extent, scale, most, cuts=(), kind=jnp.bfloat16):
    values = scale * jax.random.normal(stream_key, extent, jnp.float32)
    if cuts:
        values = values * block_scale(stream_key, extent, cuts, -0.22, 0.18)
    return jnp.clip(values, -most, most).astype(kind)


def setup_inputs(seed: int = 0) -> dict:
    keys = jax.random.split(jax.random.key(seed), 5)
    elementals = centred(keys[0], (NT, MOM, 2, N, N), (2 * N) ** -0.5, 0.25, ((0, 16), (1, 8)))
    perambulators = centred(keys[1], (NSRC, NT, 2, N, N), (2 * N) ** -0.5, 0.25, ((0, 8), (1, 16)), jnp.float32)
    source_times = draw_source_times(jax.random.fold_in(keys[4], 71), 0)
    pair_index = draw_pair_index(jax.random.fold_in(keys[4], 71), 0)
    return dict(elementals=elementals, perambulators=perambulators, source_times=source_times, pair_index=pair_index)


def contract(former, latter, form):
    return jnp.einsum(form, former, latter, precision=lax.Precision.HIGHEST)


def complex_product(former, latter, form, axis):
    former_real, former_imaginary = former[..., 0, :, :], former[..., 1, :, :]
    latter_real, latter_imaginary = latter[..., 0, :, :], latter[..., 1, :, :]
    product_real = contract(former_real, latter_real, form) - contract(former_imaginary, latter_imaginary, form)
    product_imaginary = contract(former_real, latter_imaginary, form) + contract(former_imaginary, latter_real, form)
    return jnp.stack([product_real, product_imaginary], axis=axis)


def conjugate_product(former, latter, form, axis):
    former_real, former_imaginary = former[..., 0, :, :], former[..., 1, :, :]
    latter_real, latter_imaginary = latter[..., 0, :, :], latter[..., 1, :, :]
    product_real = contract(former_real, latter_real, form) + contract(former_imaginary, latter_imaginary, form)
    product_imaginary = contract(former_imaginary, latter_real, form) - contract(former_real, latter_imaginary, form)
    return jnp.stack([product_real, product_imaginary], axis=axis)


def complex_times(former, latter):
    return jnp.stack([former[0] * latter[0] - former[1] * latter[1], former[0] * latter[1] + former[1] * latter[0]], axis=0)


def to_bf16(values):
    return values.astype(jnp.bfloat16).astype(jnp.float32)


def diagrams(sink_chain, source_chain, first_mom, second_mom):
    table = conjugate_product(sink_chain, source_chain, "aij,cij->ac", 0)
    box_value = complex_times(table[:, first_mom, first_mom], table[:, second_mom, second_mom])
    box_value = box_value - complex_times(table[:, first_mom, second_mom], table[:, second_mom, first_mom])
    sink_first = jnp.take(sink_chain, first_mom, axis=0)
    sink_second = jnp.take(sink_chain, second_mom, axis=0)
    source_first = jnp.take(source_chain, first_mom, axis=0)
    source_second = jnp.take(source_chain, second_mom, axis=0)
    loop_aa = to_bf16(conjugate_product(sink_first, source_first, "kij,klj->kil", -3))
    loop_bb = to_bf16(conjugate_product(sink_second, source_second, "kij,klj->kil", -3))
    loop_ab = to_bf16(conjugate_product(sink_first, source_second, "kij,klj->kil", -3))
    loop_ba = to_bf16(conjugate_product(sink_second, source_first, "kij,klj->kil", -3))
    cross_value = complex_product(loop_aa, loop_bb, "kij,kji->k", 0) - complex_product(loop_ab, loop_ba, "kij,kji->k", 0)
    return box_value, cross_value


def reference(elementals, perambulators, source_times, pair_index):
    phases = elementals.astype(jnp.float32)
    first_mom = pair_index[:, 0]
    second_mom = pair_index[:, 1]

    def block(position):
        slot = position // NT
        sink = position % NT
        propagator = to_bf16(perambulators[slot, sink])
        sink_phase = phases[sink]
        source_phase = phases[source_times[slot]]
        sink_chain = to_bf16(complex_product(sink_phase, propagator, "mij,jk->mik", -3))
        source_chain = to_bf16(complex_product(propagator, source_phase, "ij,mjk->mik", -3))
        return diagrams(sink_chain, source_chain, first_mom, second_mom)

    box_all, cross_all = lax.map(block, jnp.arange(NSRC * NT, dtype=jnp.int32))
    box_all = jnp.transpose(box_all.reshape(NSRC, NT, 2, PAIRS), (2, 3, 0, 1))
    cross_all = jnp.transpose(cross_all.reshape(NSRC, NT, 2, PAIRS), (2, 3, 0, 1))
    return box_all, cross_all
```

```python
import functools

import jax
import jax.numpy as jnp
from jax import lax
from jax.experimental import pallas as pl
from jax.experimental.pallas import tpu as pltpu
from jax.sharding import PartitionSpec as P

BF = jnp.bfloat16
F32 = jnp.float32
MESH = pl.DeviceIdType.MESH
N = 256
G = 64
HM = (G + N) // 2
NN = (((1,), (0,)), ((), ()))
NT = (((1,), (1,)), ((), ()))
TN = (((0,), (0,)), ((), ()))


def mm(form, a, b):
    return lax.dot_general(a, b, form, preferred_element_type=F32)


def kernel(
    times,
    pairs,
    e_ref,
    p_ref,
    box_ref,
    cross_ref,
    ebuf,
    abuf,
    bsel,
    fbuf,
    pw,
    pleft,
    sb,
    rb,
    lb,
    lt,
    mb,
    mt,
    cacc,
    tab,
    e_send,
    e_recv,
    a_send,
    a_recv,
    b_send,
    b_recv,
    c_send,
    c_recv,
    k_send,
    k_recv,
):
    s = lax.axis_index("src")
    k = lax.axis_index("snk")
    x, yl = s // 2, s % 2
    z, yh, core = k // 4, (k // 2) % 2, k % 2
    s_par = x * 2 + (1 - yl)
    s_right = ((x + 1) % 4) * 2 + yl
    s_left = ((x + 3) % 4) * 2 + yl
    s_opp = ((x + 2) % 4) * 2 + yl

    def other(m):
        return (m // 2) * 2 + (1 - m % 2)

    right, left, ypar = (s_right, k), (s_left, k), (s_par, k)

    barrier = pltpu.get_barrier_semaphore()
    for d in range(1, 16):
        pl.semaphore_signal(barrier, 1, device_id=(s, (k + d) % 16), device_id_type=MESH)
    for d in range(1, 8):
        pl.semaphore_signal(barrier, 1, device_id=((s + d) % 8, k), device_id_type=MESH)
    pl.semaphore_wait(barrier, 22)

    def rows(ref, lo, hi):
        return ref.at[:, pl.ds(lo, hi - lo), :]

    def e_msg(t, j):
        own = e_ref.at[t, 0]
        table = [
            (own, s, G, N, ypar),
            (own, s, G, N, right),
            (own, s, G, N, left),
            (None, s_par, G, N, right),
            (None, s_par, G, N, left),
            (None, s_left, G, HM, right),
            (None, s_right, HM, N, left),
            (None, other(s_left), G, HM, right),
            (None, other(s_right), HM, N, left),
            (own, s, 0, G, right),
            (own, s, 0, G, left),
            (None, s_left, 0, G // 2, right),
            (None, s_right, G // 2, G, left),
            (own, s, 0, G, ypar),
            (None, s_left, 0, G, ypar),
            (None, s_right, 0, G, ypar),
            (None, s_opp, 0, G, ypar),
        ]
        src, m, lo, hi, dev = table[j]
        dst = ebuf.at[t, m]
        src = dst if src is None else src
        return pltpu.make_async_remote_copy(
            rows(src, lo, hi),
            rows(dst, lo, hi),
            e_send.at[t, j],
            e_recv.at[t, j],
            device_id=dev,
            device_id_type=MESH,
        )

    def go(t, *js):
        for j in js:
            e_msg(t, j).start()

    def got(t, *js):
        for j in js:
            e_msg(t, j).wait_recv()

    def chunk(q):
        return pl.ds(pl.multiple_of(q * 16, 16), 16)

    def a_msg(d):
        q = (k + d) % 16
        return pltpu.make_async_remote_copy(
            e_ref.at[:, 0, :, chunk(q), :],
            abuf.at[pl.ds(2 * k, 2)],
            a_send,
            a_recv,
            device_id=(s, q),
            device_id_type=MESH,
        )

    def b_msg(d):
        q = (s + d) % 8
        return pltpu.make_async_remote_copy(
            bsel.at[q],
            fbuf.at[s, :, chunk(k), :],
            b_send,
            b_recv,
            device_id=(q, k),
            device_id_type=MESH,
        )

    def snk(zz, hh, cc):
        return (zz * 2 + hh) * 2 + cc

    zr, zl, zo, hp = (z + 1) % 4, (z + 3) % 4, (z + 2) % 4, 1 - yh
    to_zr, to_zl = (s, snk(zr, yh, core)), (s, snk(zl, yh, core))
    to_hp, to_core = (s, snk(z, hp, core)), (s, snk(z, yh, 1 - core))

    def c_msg(j):
        table = [
            (snk(z, yh, core), 0, 8, to_hp),
            (snk(z, yh, core), 0, 8, to_zr),
            (snk(z, yh, core), 0, 8, to_zl),
            (snk(z, hp, core), 0, 8, to_zr),
            (snk(z, hp, core), 0, 8, to_zl),
            (snk(zl, yh, core), 0, 4, to_zr),
            (snk(zr, yh, core), 4, 8, to_zl),
            (snk(zl, hp, core), 0, 4, to_zr),
            (snk(zr, hp, core), 4, 8, to_zl),
        ]
        q, lo, hi, dev = table[j]
        ref = fbuf.at[pl.ds(lo, hi - lo), :, chunk(q), :]
        return pltpu.make_async_remote_copy(
            ref, ref, c_send.at[j], c_recv.at[j], device_id=dev, device_id_type=MESH
        )

    def k_msg(j):
        table = [(z, yh), (z, hp), (zl, yh), (zr, yh), (zl, hp), (zr, hp), (zo, yh), (zo, hp)]
        zz, hh = table[j]
        ref = fbuf.at[:, :, chunk(snk(zz, hh, core)), :]
        return pltpu.make_async_remote_copy(
            ref, ref, k_send.at[j], k_recv.at[j], device_id=to_core, device_id_type=MESH
        )

    def put_s(u, m, real, imaginary):
        real = real.astype(BF)
        sb[u, m, 0] = real
        sb[u, m, 1] = imaginary.astype(BF)
        sb[u, m, 2] = -real

    def sink_chain(u, m, ref):
        both = jnp.concatenate([ref[0], ref[1]], axis=1)
        put_s(u, m, mm(NN, both, pw[u, :, 0:N]), mm(NN, both, pw[u, :, N : 2 * N]))

    def source_chain(m):
        both = jnp.concatenate([fbuf[m, 0], fbuf[m, 1]], axis=0)
        out = mm(NN, pleft[...], both).astype(BF)
        for u in range(2):
            for c in range(2):
                rb[u, m, c] = out[(2 * u + c) * N : (2 * u + c + 1) * N]

    def loops(u, m):
        sr, si, sn = sb[u, m, 0], sb[u, m, 1], sb[u, m, 2]
        rr, ri = rb[u, m, 0], rb[u, m, 1]
        r_row = jnp.concatenate([rr, ri], axis=1)
        r_col = jnp.concatenate([rr, ri], axis=0)
        for c, (one, two) in enumerate(((sr, si), (si, sn))):
            out = mm(NT, jnp.concatenate([one, two], axis=1), r_row).astype(BF)
            lb[m, c] = out
            lt[m, c] = out.T
        for c, (one, two) in enumerate(((sr, si), (si, sn))):
            out = mm(TN, r_col, jnp.concatenate([one, two], axis=0)).astype(BF)
            mb[m, c] = out
            mt[m, c] = out.T

    def crossed(u):
        def pair(n, carry):
            a, b = pairs[n, 0], pairs[n, 1]

            def body(i, acc):
                re, im = acc
                r = pl.ds(pl.multiple_of(i * 16, 16), 16)
                for one, two, sign in ((lb, lt, 1.0), (mb, mt, -1.0)):
                    ar, ai = one[a, 0, r, :].astype(F32), one[a, 1, r, :].astype(F32)
                    br, bi = two[b, 0, r, :].astype(F32), two[b, 1, r, :].astype(F32)
                    if sign > 0:
                        re = re + (ar * br - ai * bi)
                        im = im + (ar * bi + ai * br)
                    else:
                        re = re - (ar * br - ai * bi)
                        im = im - (ar * bi + ai * br)
                return re, im

            zero = jnp.zeros((16, N), F32)
            sums = lax.fori_loop(0, 16, body, (zero, zero), unroll=4)
            for c in range(2):
                v = sums[c]
                v = v[0:8] + v[8:16]
                cacc[u, c, n] = v[:, 0:128] + v[:, 128:256]
            return carry

        lax.fori_loop(0, 8, pair, 0)

    def trace_table(u):
        def side(ref, i):
            r = pl.ds(i * 16, 16)
            return jnp.concatenate(
                [ref[u, :, c, r, :].reshape(128, N) for c in range(2)], axis=0
            )

        total = mm(
            NT,
            jnp.concatenate([side(sb, i) for i in range(16)], axis=1),
            jnp.concatenate([side(rb, i) for i in range(16)], axis=1),
        )
        real = total[0:128, 0:128] + total[128:256, 128:256]
        imaginary = total[128:256, 0:128] - total[0:128, 128:256]
        row = lax.broadcasted_iota(jnp.int32, (128, 128), 0) % 16
        col = lax.broadcasted_iota(jnp.int32, (128, 128), 1) % 16
        for c, part in enumerate((real, imaginary)):
            part = jnp.where(row == col, part, 0.0)
            tab[u, c] = jnp.sum(part.reshape(8, 16, 128), axis=1)

    def finish():
        sub = lax.broadcasted_iota(jnp.int32, (8, 128), 0)
        lane = lax.broadcasted_iota(jnp.int32, (8, 128), 1) // 16
        first = jnp.zeros((8, 128), jnp.int32)
        second = jnp.zeros((8, 128), jnp.int32)
        for n in range(8):
            first = jnp.where(sub == n, pairs[n, 0], first)
            second = jnp.where(sub == n, pairs[n, 1], second)

        def pick(table, one, two):
            got_rows = jnp.zeros((8, 128), F32)
            for m in range(8):
                got_rows = got_rows + jnp.where(one == m, table[m : m + 1, :], 0.0)
            return jnp.sum(jnp.where(lane == two, got_rows, 0.0), axis=1, keepdims=True)

        boxes, crosses = [], []
        for u in range(2):
            val = []
            for one, two in ((first, first), (second, second), (first, second), (second, first)):
                val.append([pick(tab[u, c], one, two) for c in range(2)])
            (ar, ai), (br, bi), (cr, ci), (dr, di) = val
            boxes.append(
                (
                    (ar * br - ai * bi) - (cr * dr - ci * di),
                    (ar * bi + ai * br) - (cr * di + ci * dr),
                )
            )
            crosses.append(
                [
                    jnp.sum(jnp.sum(cacc[u, c], axis=1), axis=1, keepdims=True)
                    for c in range(2)
                ]
            )
        for c in range(2):
            box_ref[c] = jnp.concatenate([boxes[0][c], boxes[1][c]], axis=1)
            cross_ref[c] = jnp.concatenate([crosses[0][c], crosses[1][c]], axis=1)

    for d in range(1, 16):
        a_msg(d).start()
    go(0, 0, 1, 2, 9, 10, 13)

    abuf[pl.ds(2 * k, 2)] = e_ref[:, 0, :, chunk(k), :]
    for u in range(2):
        real = p_ref[0, u, 0].astype(BF)
        imaginary = p_ref[0, u, 1].astype(BF)
        pw[u, 0:N, 0:N] = real
        pw[u, 0:N, N : 2 * N] = imaginary
        pw[u, N : 2 * N, 0:N] = -imaginary
        pw[u, N : 2 * N, N : 2 * N] = real
        base = 2 * u * N
        pleft[base : base + N, 0:N] = real
        pleft[base : base + N, N : 2 * N] = -imaginary
        pleft[base + N : base + 2 * N, 0:N] = imaginary
        pleft[base + N : base + 2 * N, N : 2 * N] = real
    for u in range(2):
        sink_chain(u, s, e_ref.at[u, 0])

    pltpu.make_async_copy(abuf.at[0:30], abuf.at[0:30], a_recv).wait()
    for n in range(8):
        bsel[n] = abuf[times[n]]
    for d in range(1, 8):
        b_msg(d).start()
    fbuf[s, :, chunk(k), :] = bsel[s]

    got(0, 0)
    go(0, 3, 4)
    pltpu.make_async_copy(bsel.at[0:7], bsel.at[0:7], b_recv).wait()
    for j in (0, 1, 2):
        c_msg(j).start()
    k_msg(0).start()
    got(0, 9)
    go(0, 11, 14)
    got(0, 10)
    go(0, 12, 15)
    got(0, 1)
    go(0, 5)
    got(0, 2)
    go(0, 6)
    go(1, 0, 1, 2, 9, 10, 13)
    c_msg(0).wait_recv()
    c_msg(3).start()
    c_msg(4).start()
    k_msg(1).start()
    got(0, 11, 12)
    go(0, 16)
    got(0, 3)
    go(0, 7)
    got(0, 4)
    go(0, 8)
    c_msg(1).wait_recv()
    c_msg(5).start()
    k_msg(2).start()
    c_msg(2).wait_recv()
    c_msg(6).start()
    k_msg(3).start()
    got(1, 0)
    go(1, 3, 4)
    c_msg(3).wait_recv()
    c_msg(7).start()
    k_msg(4).start()
    c_msg(4).wait_recv()
    c_msg(8).start()
    k_msg(5).start()
    got(1, 9)
    go(1, 11, 14)
    got(1, 10)
    go(1, 12, 15)
    c_msg(5).wait_recv()
    c_msg(6).wait_recv()
    k_msg(6).start()
    c_msg(7).wait_recv()
    c_msg(8).wait_recv()
    k_msg(7).start()
    got(0, 13, 14, 15, 16, 5, 6, 7, 8)
    for j in range(8):
        k_msg(j).wait_recv()

    def place(j):
        dx = jnp.where(j // 2 == 1, 3, jnp.where(j // 2 == 2, 1, jnp.where(j // 2 == 3, 2, 0)))
        return ((x + dx) % 4) * 2 + (yl + j % 2) % 2

    @pl.loop(0, 8)
    def _(j):
        m = place(j)

        @pl.when(j == 1)
        def _():
            got(1, 1)
            go(1, 5)

        @pl.when(j == 2)
        def _():
            got(1, 2)
            go(1, 6)

        @pl.when(j == 3)
        def _():
            got(1, 11, 12)
            go(1, 16)

        @pl.when(j == 4)
        def _():
            got(1, 3)
            go(1, 7)

        @pl.when(j == 5)
        def _():
            got(1, 4)
            go(1, 8)

        source_chain(m)

        @pl.when(j > 0)
        def _():
            sink_chain(0, m, ebuf.at[0, m])

        loops(0, m)

    crossed(0)
    trace_table(0)

    @pl.loop(0, 8)
    def _(j):
        m = place(j)

        @pl.when(j == 1)
        def _():
            got(1, 13)

        @pl.when(j == 3)
        def _():
            got(1, 14)

        @pl.when(j == 5)
        def _():
            got(1, 15)

        @pl.when(j == 6)
        def _():
            got(1, 5, 6)

        @pl.when(j == 7)
        def _():
            got(1, 7, 8, 16)

        @pl.when(j > 0)
        def _():
            sink_chain(1, m, ebuf.at[1, m])

        loops(1, m)

    crossed(1)
    trace_table(1)
    finish()

    pltpu.make_async_copy(abuf.at[0:30], abuf.at[0:30], a_send).wait()
    pltpu.make_async_copy(bsel.at[0:7], bsel.at[0:7], b_send).wait()
    for t in range(2):
        for j in range(17):
            e_msg(t, j).wait_send()
    for j in range(9):
        c_msg(j).wait_send()
    for j in range(8):
        k_msg(j).wait_send()


def local(elementals, perambulators, source_times, pair_index):
    vm = pl.BlockSpec(memory_space=pltpu.VMEM)
    sm = pl.BlockSpec(memory_space=pltpu.SMEM)
    dma = pltpu.SemaphoreType.DMA
    boxes, crossed = pl.pallas_call(
        kernel,
        out_shape=(
            jax.ShapeDtypeStruct((2, 8, 2), F32),
            jax.ShapeDtypeStruct((2, 8, 2), F32),
        ),
        in_specs=[sm, sm, vm, vm],
        out_specs=(vm, vm),
        scratch_shapes=[
            pltpu.VMEM((2, 8, 2, N, N), BF),
            pltpu.VMEM((32, 2, 16, N), BF),
            pltpu.VMEM((8, 2, 16, N), BF),
            pltpu.VMEM((8, 2, N, N), BF),
            pltpu.VMEM((2, 2 * N, 2 * N), BF),
            pltpu.VMEM((4 * N, 2 * N), BF),
            pltpu.VMEM((2, 8, 3, N, N), BF),
            pltpu.VMEM((2, 8, 2, N, N), BF),
            pltpu.VMEM((8, 2, N, N), BF),
            pltpu.VMEM((8, 2, N, N), BF),
            pltpu.VMEM((8, 2, N, N), BF),
            pltpu.VMEM((8, 2, N, N), BF),
            pltpu.VMEM((2, 2, 8, 8, 128), F32),
            pltpu.VMEM((2, 2, 8, 128), F32),
            dma((2, 17)),
            dma((2, 17)),
            dma,
            dma,
            dma,
            dma,
            dma((9,)),
            dma((9,)),
            dma((8,)),
            dma((8,)),
        ],
        compiler_params=pltpu.CompilerParams(
            collective_id=0, has_side_effects=True, vmem_limit_bytes=56 * 1024 * 1024
        ),
        name="diagrams",
    )(source_times, pair_index, elementals, perambulators)
    return boxes[:, :, None, :], crossed[:, :, None, :]


def solution(mesh):
    return jax.shard_map(
        local,
        mesh=mesh,
        in_specs=(P("snk", "src", None, None, None), P("src", "snk", None, None, None), P(), P()),
        out_specs=(P(None, None, "src", "snk"), P(None, None, "src", "snk")),
        check_vma=False,
    )
```

```python
import functools

import jax
import jax.numpy as jnp
from jax import lax
from jax.experimental import pallas as pl
from jax.experimental.pallas import tpu as pltpu
from jax.sharding import PartitionSpec as P

BF = jnp.bfloat16
F32 = jnp.float32
MESH = pl.DeviceIdType.MESH
N = 256
G = 80
GM, HM = 32, 176
NN = (((1,), (0,)), ((), ()))
NT = (((1,), (1,)), ((), ()))
TN = (((0,), (0,)), ((), ()))


def mm(form, a, b):
    return lax.dot_general(a, b, form, preferred_element_type=F32)


def kernel(
    times,
    pairs,
    e_in,
    p_in,
    box_ref,
    cross_ref,
    ebuf,
    pbuf,
    abuf_r,
    abuf_i,
    bsel,
    fbuf,
    pw,
    ph,
    vb,
    lb,
    lt,
    mb,
    mt,
    cacc,
    tab,
    in_sem,
    e_send,
    e_recv,
    a_send,
    a_recv,
    b_send,
    b_recv,
    c_send,
    c_recv,
    k_send,
    k_recv,
):
    abuf = (abuf_r, abuf_i)
    s = lax.axis_index("src")
    k = lax.axis_index("snk")
    x, yl = s // 2, s % 2
    z, yh, core = k // 4, (k // 2) % 2, k % 2
    s_par = x * 2 + (1 - yl)
    s_right = ((x + 1) % 4) * 2 + yl
    s_left = ((x + 3) % 4) * 2 + yl
    s_opp = ((x + 2) % 4) * 2 + yl

    def other(m):
        return (m // 2) * 2 + (1 - m % 2)

    right, left, ypar = (s_right, k), (s_left, k), (s_par, k)

    khp = (z * 2 + (1 - yh)) * 2 + core

    barrier = pltpu.get_barrier_semaphore()
    for d in range(1, 16):
        pl.semaphore_signal(barrier, 1, device_id=(s, (k + d) % 16), device_id_type=MESH)
    for d in range(1, 8):
        for q in (k, khp):
            pl.semaphore_signal(barrier, 1, device_id=((s + d) % 8, q), device_id_type=MESH)

    def in_copy(n):
        if n < 2:
            return pltpu.make_async_copy(e_in.at[n, 0], ebuf.at[n, s], in_sem.at[n])
        return pltpu.make_async_copy(p_in.at[0], pbuf, in_sem.at[2])

    for n in range(3):
        in_copy(n).start()
    in_copy(0).wait()
    in_copy(1).wait()
    pl.semaphore_wait(barrier, 29)

    def rows(ref, lo, hi):
        return ref.at[:, pl.ds(lo, hi - lo), :]

    def e_msg(t, j):
        own = ebuf.at[t, s]
        table = [
            (own, s, G, N, ypar),
            (own, s, G, N, right),
            (own, s, G, N, left),
            (None, s_par, G, N, right),
            (None, s_par, G, N, left),
            (None, s_left, G, HM, right),
            (None, s_right, HM, N, left),
            (None, other(s_left), G, HM, right),
            (None, other(s_right), HM, N, left),
            (own, s, 0, G, right),
            (own, s, 0, G, left),
            (None, s_left, 0, GM, right),
            (None, s_right, GM, G, left),
            (own, s, 0, G, ypar),
            (None, s_left, 0, G, ypar),
            (None, s_right, 0, G, ypar),
            (None, s_opp, 0, G, ypar),
        ]
        src, m, lo, hi, dev = table[j]
        dst = ebuf.at[t, m]
        src = dst if src is None else src
        return pltpu.make_async_remote_copy(
            rows(src, lo, hi),
            rows(dst, lo, hi),
            e_send.at[t, j],
            e_recv.at[t, j],
            device_id=dev,
            device_id_type=MESH,
        )

    def go(t, *js):
        for j in js:
            e_msg(t, j).start()

    def got(t, *js):
        for j in js:
            e_msg(t, j).wait_recv()

    def place_of(q):
        return (q % 2) * 8 + q // 2

    def chunk(q):
        return pl.ds(pl.multiple_of(place_of(q) * 16, 16), 16)

    def chunks(zz, cc):
        return pl.ds(pl.multiple_of(cc * 128 + zz * 32, 32), 32)

    def a_msg(h, d):
        q = (k + d) % 16
        return pltpu.make_async_remote_copy(
            ebuf.at[:, s, h, chunk(q), :],
            abuf[h].at[pl.ds(2 * k, 2)],
            a_send.at[h],
            a_recv.at[h],
            device_id=(s, q),
            device_id_type=MESH,
        )

    def b_msg(h, d, far):
        q = (s + d) % 8
        return pltpu.make_async_remote_copy(
            bsel.at[h, q],
            fbuf.at[s, h, chunk(k), :],
            b_send.at[h],
            b_recv.at[h],
            device_id=(q, khp if far else k),
            device_id_type=MESH,
        )

    zr, zl, zo = (z + 1) % 4, (z + 3) % 4, (z + 2) % 4
    to_zr, to_zl = (s, (zr * 2 + yh) * 2 + core), (s, (zl * 2 + yh) * 2 + core)
    to_core = (s, (z * 2 + yh) * 2 + 1 - core)

    def c_msg(h, j):
        zz, lo, dev = [
            (z, 0, to_zr),
            (z, 4, to_zl),
            (z, 4, to_zr),
            (z, 0, to_zl),
            (zl, 0, to_zr),
            (zr, 4, to_zl),
        ][j]
        ref = fbuf.at[pl.ds(lo, 4), h, chunks(zz, core), :]
        return pltpu.make_async_remote_copy(
            ref, ref, c_send.at[h, j], c_recv.at[h, j], device_id=dev, device_id_type=MESH
        )

    def k_msg(h, j):
        zz, lo, count = [(z, 0, 8), (zl, 0, 8), (zr, 0, 8), (zo, 0, 4), (zo, 4, 4)][j]
        ref = fbuf.at[pl.ds(lo, count), h, chunks(zz, core), :]
        return pltpu.make_async_remote_copy(
            ref, ref, k_send.at[h, j], k_recv.at[h, j], device_id=to_core, device_id_type=MESH
        )

    def chain(u, *ms):
        lhs = jnp.concatenate(
            [jnp.concatenate([ebuf[u, m, 0], ebuf[u, m, 1]], axis=1) for m in ms], axis=0
        )
        out = mm(NN, lhs, pw[u]).astype(BF)
        rhs = [
            jnp.concatenate([out[i * N : (i + 1) * N, c * N : (c + 1) * N] for c in range(2)], axis=0)
            for i in range(len(ms))
        ]
        out = mm(NN, ph[u], jnp.concatenate(rhs, axis=1)).astype(BF)
        for i, m in enumerate(ms):
            real, imaginary = (out[c * N : (c + 1) * N, i * N : (i + 1) * N] for c in range(2))
            vb[u, m, 0] = real
            vb[u, m, 1] = imaginary
            vb[u, m, 2] = -real

    def loops(u, m):
        vr, vi, vn = vb[u, m, 0], vb[u, m, 1], vb[u, m, 2]
        fr, fi = fbuf[m, 0], fbuf[m, 1]
        f_row = jnp.concatenate([fr, fi], axis=1)
        f_col = jnp.concatenate([fr, fi], axis=0)
        for c, (one, two) in enumerate(((vr, vi), (vi, vn))):
            out = mm(NT, jnp.concatenate([one, two], axis=1), f_row).astype(BF)
            lb[u, m, c] = out
            lt[u, m, c] = out.T
        for c, (one, two) in enumerate(((vr, vi), (vi, vn))):
            out = mm(TN, f_col, jnp.concatenate([one, two], axis=0)).astype(BF)
            mb[u, m, c] = out
            mt[u, m, c] = out.T

    def crossed(u, n):
        a, b = pairs[0, n], pairs[1, n]
        re = jnp.zeros((16, N), F32)
        im = jnp.zeros((16, N), F32)
        for i in range(16):
            r = pl.ds(i * 16, 16)
            for one, two, sign in ((lb, lt, 1.0), (mb, mt, -1.0)):
                ar, ai = one[u, a, 0, r, :].astype(F32), one[u, a, 1, r, :].astype(F32)
                br, bi = two[u, b, 0, r, :].astype(F32), two[u, b, 1, r, :].astype(F32)
                if sign > 0:
                    re = re + (ar * br - ai * bi)
                    im = im + (ar * bi + ai * br)
                else:
                    re = re - (ar * br - ai * bi)
                    im = im - (ar * bi + ai * br)
        for c, v in enumerate((re, im)):
            v = v[0:8] + v[8:16]
            cacc[u, c, n] = v[:, 0:128] + v[:, 128:256]

    def trace_table(u):
        def side(ref, i):
            r = pl.ds(i * 16, 16)
            return jnp.concatenate([ref[:, c, r, :].reshape(128, N) for c in range(2)], axis=0)

        total = mm(
            NT,
            jnp.concatenate([side(vb.at[u], i) for i in range(16)], axis=1),
            jnp.concatenate([side(fbuf, i) for i in range(16)], axis=1),
        )
        real = total[0:128, 0:128] + total[128:256, 128:256]
        imaginary = total[128:256, 0:128] - total[0:128, 128:256]
        row = lax.broadcasted_iota(jnp.int32, (128, 128), 0) % 16
        col = lax.broadcasted_iota(jnp.int32, (128, 128), 1) % 16
        for c, part in enumerate((real, imaginary)):
            part = jnp.where(row == col, part, 0.0)
            tab[u, c] = jnp.sum(part.reshape(8, 16, 128), axis=1)

    def finish():
        sub = lax.broadcasted_iota(jnp.int32, (8, 128), 0)
        lane = lax.broadcasted_iota(jnp.int32, (8, 128), 1) // 16
        first = jnp.zeros((8, 128), jnp.int32)
        second = jnp.zeros((8, 128), jnp.int32)
        for n in range(8):
            first = jnp.where(sub == n, pairs[0, n], first)
            second = jnp.where(sub == n, pairs[1, n], second)

        def pick(table, one, two):
            got_rows = jnp.zeros((8, 128), F32)
            for m in range(8):
                got_rows = got_rows + jnp.where(one == m, table[m : m + 1, :], 0.0)
            return jnp.sum(jnp.where(lane == two, got_rows, 0.0), axis=1, keepdims=True)

        spot = lax.broadcasted_iota(jnp.int32, (8, 128), 1) == sub

        def along(column):
            return jnp.sum(jnp.where(spot, column, 0.0), axis=0, keepdims=True)[:, 0:8]

        for u in range(2):
            val = []
            for one, two in ((first, first), (second, second), (first, second), (second, first)):
                val.append([pick(tab[u, c], one, two) for c in range(2)])
            (ar, ai), (br, bi), (cr, ci), (dr, di) = val
            box = (
                (ar * br - ai * bi) - (cr * dr - ci * di),
                (ar * bi + ai * br) - (cr * di + ci * dr),
            )
            for c in range(2):
                cross = jnp.sum(jnp.sum(cacc[u, c], axis=1), axis=1, keepdims=True)
                box_ref[c, u : u + 1, :] = along(box[c])
                cross_ref[c, u : u + 1, :] = along(cross)

    def all_of(sem, count):
        ref = abuf_r.at[pl.ds(0, count)]
        return pltpu.make_async_copy(ref, ref, sem)

    a_all = [all_of(a_recv.at[h], 30) for h in range(2)]
    a_out = [all_of(a_send.at[h], 30) for h in range(2)]
    b_all = [all_of(b_recv.at[h], 15) for h in range(2)]
    b_out = [all_of(b_send.at[h], 15) for h in range(2)]

    def choose(h):
        abuf[h][pl.ds(2 * k, 2)] = ebuf[:, s, h, chunk(k), :]
        a_all[h].wait()
        for n in range(8):
            bsel[h, n] = abuf[h][times[n]]
        for d in range(1, 8):
            b_msg(h, d, True).start()
            b_msg(h, d, False).start()
        b_msg(h, 0, True).start()
        fbuf[s, h, chunk(k), :] = bsel[h, s]

    def spread(h):
        b_all[h].wait()
        for j in (0, 1, 2, 3):
            c_msg(h, j).start()
        k_msg(h, 0).start()

    def c_got(h, j):
        c_msg(h, j).wait_recv()

    for h in range(2):
        for d in range(1, 16):
            a_msg(h, d).start()
    go(0, 9, 10)
    go(1, 9, 10)
    go(0, 1, 2)

    in_copy(2).wait()
    for u in range(2):
        real = pbuf[u, 0].astype(BF)
        imaginary = pbuf[u, 1].astype(BF)
        pw[u, 0:N, 0:N] = real
        pw[u, 0:N, N : 2 * N] = imaginary
        pw[u, N : 2 * N, 0:N] = -imaginary
        pw[u, N : 2 * N, N : 2 * N] = real
        ph[u, 0:N, 0:N] = real.T
        ph[u, 0:N, N : 2 * N] = imaginary.T
        ph[u, N : 2 * N, 0:N] = (-imaginary).T
        ph[u, N : 2 * N, N : 2 * N] = real.T

    choose(0)
    got(0, 9, 10)
    go(0, 11, 12)
    got(1, 9, 10)
    go(1, 11, 12)
    go(0, 0)
    choose(1)
    go(1, 1, 2)
    got(0, 1)
    go(0, 5)
    got(0, 2)
    go(0, 6)
    go(0, 13, 14, 15)
    go(1, 0)
    spread(0)
    chain(0, s, s_left, s_right)
    got(0, 0)
    go(0, 3, 4)
    got(0, 11, 12)
    go(0, 16)
    spread(1)
    got(1, 1)
    go(1, 5)
    got(1, 2)
    go(1, 6)
    c_got(0, 0)
    c_msg(0, 4).start()
    c_got(0, 1)
    c_msg(0, 5).start()
    c_got(0, 2)
    k_msg(0, 1).start()
    c_got(0, 3)
    k_msg(0, 2).start()
    chain(1, s, s_left, s_right)
    got(1, 0)
    go(1, 3, 4)
    c_got(1, 0)
    c_msg(1, 4).start()
    c_got(1, 1)
    c_msg(1, 5).start()
    c_got(1, 2)
    k_msg(1, 1).start()
    c_got(1, 3)
    k_msg(1, 2).start()
    got(0, 3)
    go(0, 7)
    got(0, 4)
    go(0, 8)
    go(1, 13, 14, 15)
    got(1, 11, 12)
    go(1, 16)
    c_got(0, 4)
    k_msg(0, 3).start()
    c_got(0, 5)
    k_msg(0, 4).start()
    got(0, 13)
    got(0, 5, 6)
    chain(0, s_par, s_opp)
    c_got(1, 4)
    k_msg(1, 3).start()
    c_got(1, 5)
    k_msg(1, 4).start()
    got(0, 14, 15)
    chain(0, other(s_left), other(s_right))
    got(1, 3)
    go(1, 7)
    got(1, 4)
    go(1, 8)
    for h in range(2):
        for j in range(5):
            k_msg(h, j).wait_recv()

    def place(j):
        q = j % 4
        dx = jnp.where(q == 1, 3, jnp.where(q == 2, 1, jnp.where(q == 3, 2, 0)))
        return ((x + dx) % 4) * 2 + (yl + j // 4) % 2

    for j in range(4):
        loops(0, place(j))
    got(0, 7, 8, 16)
    chain(0, other(s_opp))
    for j in range(4, 8):
        loops(0, place(j))
    trace_table(0)
    got(1, 5, 6)
    got(1, 13)
    chain(1, s_opp, s_par)
    for j in range(4):
        loops(1, place(j))
        crossed(0, j)
    got(1, 14, 15)
    chain(1, other(s_left), other(s_right))
    for j in range(4, 7):
        loops(1, place(j))
        crossed(0, j)
    got(1, 7, 8, 16)
    chain(1, other(s_opp))
    loops(1, place(7))
    crossed(0, 7)
    trace_table(1)

    @pl.loop(0, 8)
    def _(n):
        crossed(1, n)

    finish()

    for h in range(2):
        a_out[h].wait()
        b_out[h].wait()
    for t in range(2):
        for j in range(17):
            e_msg(t, j).wait_send()
    for h in range(2):
        for j in range(6):
            c_msg(h, j).wait_send()
        for j in range(5):
            k_msg(h, j).wait_send()


def local(elementals, perambulators, source_times, pair_index):
    vm = pl.BlockSpec(memory_space=pltpu.VMEM)
    sm = pl.BlockSpec(memory_space=pltpu.SMEM)
    hbm = pl.BlockSpec(memory_space=pl.ANY)
    dma = pltpu.SemaphoreType.DMA
    boxes, crossed = pl.pallas_call(
        kernel,
        out_shape=(
            jax.ShapeDtypeStruct((2, 2, 8), F32),
            jax.ShapeDtypeStruct((2, 2, 8), F32),
        ),
        in_specs=[sm, sm, hbm, hbm],
        out_specs=(vm, vm),
        scratch_shapes=[
            pltpu.VMEM((2, 8, 2, N, N), BF),
            pltpu.VMEM((2, 2, N, N), F32),
            pltpu.VMEM((32, 16, N), BF),
            pltpu.VMEM((32, 16, N), BF),
            pltpu.VMEM((2, 8, 16, N), BF),
            pltpu.VMEM((8, 2, N, N), BF),
            pltpu.VMEM((2, 2 * N, 2 * N), BF),
            pltpu.VMEM((2, 2 * N, 2 * N), BF),
            pltpu.VMEM((2, 8, 3, N, N), BF),
            pltpu.VMEM((2, 8, 2, N, N), BF),
            pltpu.VMEM((2, 8, 2, N, N), BF),
            pltpu.VMEM((2, 8, 2, N, N), BF),
            pltpu.VMEM((2, 8, 2, N, N), BF),
            pltpu.VMEM((2, 2, 8, 8, 128), F32),
            pltpu.VMEM((2, 2, 8, 128), F32),
            dma((3,)),
            dma((2, 17)),
            dma((2, 17)),
            dma((2,)),
            dma((2,)),
            dma((2,)),
            dma((2,)),
            dma((2, 6)),
            dma((2, 6)),
            dma((2, 5)),
            dma((2, 5)),
        ],
        compiler_params=pltpu.CompilerParams(
            collective_id=0, has_side_effects=True, vmem_limit_bytes=56 * 1024 * 1024
        ),
        name="diagrams",
    )(source_times, pair_index.T, elementals, perambulators)
    return tuple(v.transpose(0, 2, 1)[:, :, None, :] for v in (boxes, crossed))


def solution(mesh):
    return jax.shard_map(
        local,
        mesh=mesh,
        in_specs=(P("snk", "src", None, None, None), P("src", "snk", None, None, None), P(), P()),
        out_specs=(P(None, None, "src", "snk"), P(None, None, "src", "snk")),
        check_vma=False,
    )
```

```python
import functools

import jax
import jax.numpy as jnp
from jax import lax
from jax.experimental import pallas as pl
from jax.experimental.pallas import tpu as pltpu
from jax.sharding import PartitionSpec as P

BF = jnp.bfloat16
F32 = jnp.float32
MESH = pl.DeviceIdType.MESH
N = 256
G = 80
GM, HM = 32, 176
NN = (((1,), (0,)), ((), ()))
NT = (((1,), (1,)), ((), ()))
TN = (((0,), (0,)), ((), ()))


def mm(form, a, b):
    return lax.dot_general(a, b, form, preferred_element_type=F32)


def kernel(
    times,
    pairs,
    e_in,
    p_in,
    box_ref,
    cross_ref,
    ebuf,
    pbuf,
    abuf_r,
    abuf_i,
    bsel,
    fbuf,
    pw,
    ph,
    vb,
    lb,
    lt,
    mb,
    mt,
    cacc,
    tab,
    in_sem,
    e_send,
    e_recv,
    a_send,
    a_recv,
    b_send,
    b_recv,
    c_send,
    c_recv,
    k_send,
    k_recv,
):
    abuf = (abuf_r, abuf_i)
    s = lax.axis_index("src")
    k = lax.axis_index("snk")
    x, yl = s // 2, s % 2
    z, yh, core = k // 4, (k // 2) % 2, k % 2
    s_par = x * 2 + (1 - yl)
    s_right = ((x + 1) % 4) * 2 + yl
    s_left = ((x + 3) % 4) * 2 + yl
    s_opp = ((x + 2) % 4) * 2 + yl

    def other(m):
        return (m // 2) * 2 + (1 - m % 2)

    right, left, ypar = (s_right, k), (s_left, k), (s_par, k)

    khp = (z * 2 + (1 - yh)) * 2 + core

    barrier = pltpu.get_barrier_semaphore()
    for d in range(1, 16):
        pl.semaphore_signal(barrier, 1, device_id=(s, (k + d) % 16), device_id_type=MESH)
    for d in range(1, 8):
        for q in (k, khp):
            pl.semaphore_signal(barrier, 1, device_id=((s + d) % 8, q), device_id_type=MESH)

    def in_copy(n):
        if n < 2:
            return pltpu.make_async_copy(e_in.at[n, 0], ebuf.at[n, s], in_sem.at[n])
        return pltpu.make_async_copy(p_in.at[0], pbuf, in_sem.at[2])

    for n in range(3):
        in_copy(n).start()
    in_copy(0).wait()
    in_copy(1).wait()
    pl.semaphore_wait(barrier, 29)

    def rows(ref, lo, hi):
        return ref.at[:, pl.ds(lo, hi - lo), :]

    def e_msg(t, j):
        own = ebuf.at[t, s]
        table = [
            (own, s, G, HM, ypar),
            (own, s, G, HM, right),
            (own, s, HM, N, left),
            (None, s_par, G, HM, right),
            (None, s_par, HM, N, left),
            (None, s_left, G, HM, right),
            (None, s_right, HM, N, left),
            (None, other(s_left), G, HM, right),
            (None, other(s_right), HM, N, left),
            (own, s, 0, G, right),
            (own, s, 0, G, left),
            (None, s_left, 0, GM, right),
            (None, s_right, GM, G, left),
            (own, s, 0, G, ypar),
            (None, s_left, 0, G, ypar),
            (None, s_right, 0, G, ypar),
            (None, s_opp, 0, G, ypar),
            (own, s, HM, N, right),
            (own, s, G, HM, left),
            (None, s_par, HM, N, right),
            (None, s_par, G, HM, left),
            (own, s, HM, N, ypar),
        ]
        src, m, lo, hi, dev = table[j]
        dst = ebuf.at[t, m]
        src = dst if src is None else src
        return pltpu.make_async_remote_copy(
            rows(src, lo, hi),
            rows(dst, lo, hi),
            e_send.at[t, j],
            e_recv.at[t, j],
            device_id=dev,
            device_id_type=MESH,
        )

    def go(t, *js):
        for j in js:
            e_msg(t, j).start()

    def got(t, *js):
        for j in js:
            e_msg(t, j).wait_recv()

    def place_of(q):
        return (q % 2) * 8 + q // 2

    def chunk(q):
        return pl.ds(pl.multiple_of(place_of(q) * 16, 16), 16)

    def chunks(zz, cc):
        return pl.ds(pl.multiple_of(cc * 128 + zz * 32, 32), 32)

    def a_msg(h, d):
        q = (k + d) % 16
        return pltpu.make_async_remote_copy(
            ebuf.at[:, s, h, chunk(q), :],
            abuf[h].at[pl.ds(2 * k, 2)],
            a_send.at[h],
            a_recv.at[h],
            device_id=(s, q),
            device_id_type=MESH,
        )

    def b_msg(h, d, far):
        q = (s + d) % 8
        return pltpu.make_async_remote_copy(
            bsel.at[h, q],
            fbuf.at[s, h, chunk(k), :],
            b_send.at[h],
            b_recv.at[h],
            device_id=(q, khp if far else k),
            device_id_type=MESH,
        )

    zr, zl, zo = (z + 1) % 4, (z + 3) % 4, (z + 2) % 4
    to_zr, to_zl = (s, (zr * 2 + yh) * 2 + core), (s, (zl * 2 + yh) * 2 + core)
    to_core = (s, (z * 2 + yh) * 2 + 1 - core)

    def c_msg(h, j):
        zz, lo, dev = [
            (z, 0, to_zr),
            (z, 4, to_zl),
            (z, 4, to_zr),
            (z, 0, to_zl),
            (zl, 0, to_zr),
            (zr, 4, to_zl),
        ][j]
        ref = fbuf.at[pl.ds(lo, 4), h, chunks(zz, core), :]
        return pltpu.make_async_remote_copy(
            ref, ref, c_send.at[h, j], c_recv.at[h, j], device_id=dev, device_id_type=MESH
        )

    def k_msg(h, j):
        zz, lo, count = [(z, 0, 8), (zl, 0, 8), (zr, 0, 8), (zo, 0, 4), (zo, 4, 4)][j]
        ref = fbuf.at[pl.ds(lo, count), h, chunks(zz, core), :]
        return pltpu.make_async_remote_copy(
            ref, ref, k_send.at[h, j], k_recv.at[h, j], device_id=to_core, device_id_type=MESH
        )

    def chain(u, *ms):
        lhs = jnp.concatenate(
            [jnp.concatenate([ebuf[u, m, 0], ebuf[u, m, 1]], axis=1) for m in ms], axis=0
        )
        out = mm(NN, lhs, pw[u]).astype(BF)
        rhs = [
            jnp.concatenate([out[i * N : (i + 1) * N, c * N : (c + 1) * N] for c in range(2)], axis=0)
            for i in range(len(ms))
        ]
        out = mm(NN, ph[u], jnp.concatenate(rhs, axis=1)).astype(BF)
        for i, m in enumerate(ms):
            real, imaginary = (out[c * N : (c + 1) * N, i * N : (i + 1) * N] for c in range(2))
            vb[u, m, 0] = real
            vb[u, m, 1] = imaginary
            vb[u, m, 2] = -real

    def loops(u, m):
        vr, vi, vn = vb[u, m, 0], vb[u, m, 1], vb[u, m, 2]
        fr, fi = fbuf[m, 0], fbuf[m, 1]
        f_row = jnp.concatenate([fr, fi], axis=1)
        f_col = jnp.concatenate([fr, fi], axis=0)
        for c, (one, two) in enumerate(((vr, vi), (vi, vn))):
            out = mm(NT, jnp.concatenate([one, two], axis=1), f_row).astype(BF)
            lb[u, m, c] = out
            lt[u, m, c] = out.T
        for c, (one, two) in enumerate(((vr, vi), (vi, vn))):
            out = mm(TN, f_col, jnp.concatenate([one, two], axis=0)).astype(BF)
            mb[u, m, c] = out
            mt[u, m, c] = out.T

    def crossed(u, n):
        a, b = pairs[0, n], pairs[1, n]
        re = jnp.zeros((16, N), F32)
        im = jnp.zeros((16, N), F32)
        for i in range(16):
            r = pl.ds(i * 16, 16)
            for one, two, sign in ((lb, lt, 1.0), (mb, mt, -1.0)):
                ar, ai = one[u, a, 0, r, :].astype(F32), one[u, a, 1, r, :].astype(F32)
                br, bi = two[u, b, 0, r, :].astype(F32), two[u, b, 1, r, :].astype(F32)
                if sign > 0:
                    re = re + (ar * br - ai * bi)
                    im = im + (ar * bi + ai * br)
                else:
                    re = re - (ar * br - ai * bi)
                    im = im - (ar * bi + ai * br)
        for c, v in enumerate((re, im)):
            v = v[0:8] + v[8:16]
            cacc[u, c, n] = v[:, 0:128] + v[:, 128:256]

    def trace_table(u):
        def side(ref, i):
            r = pl.ds(i * 16, 16)
            return jnp.concatenate([ref[:, c, r, :].reshape(128, N) for c in range(2)], axis=0)

        total = mm(
            NT,
            jnp.concatenate([side(vb.at[u], i) for i in range(16)], axis=1),
            jnp.concatenate([side(fbuf, i) for i in range(16)], axis=1),
        )
        real = total[0:128, 0:128] + total[128:256, 128:256]
        imaginary = total[128:256, 0:128] - total[0:128, 128:256]
        row = lax.broadcasted_iota(jnp.int32, (128, 128), 0) % 16
        col = lax.broadcasted_iota(jnp.int32, (128, 128), 1) % 16
        for c, part in enumerate((real, imaginary)):
            part = jnp.where(row == col, part, 0.0)
            tab[u, c] = jnp.sum(part.reshape(8, 16, 128), axis=1)

    def finish():
        sub = lax.broadcasted_iota(jnp.int32, (8, 128), 0)
        lane = lax.broadcasted_iota(jnp.int32, (8, 128), 1) // 16
        first = jnp.zeros((8, 128), jnp.int32)
        second = jnp.zeros((8, 128), jnp.int32)
        for n in range(8):
            first = jnp.where(sub == n, pairs[0, n], first)
            second = jnp.where(sub == n, pairs[1, n], second)

        def pick(table, one, two):
            got_rows = jnp.zeros((8, 128), F32)
            for m in range(8):
                got_rows = got_rows + jnp.where(one == m, table[m : m + 1, :], 0.0)
            return jnp.sum(jnp.where(lane == two, got_rows, 0.0), axis=1, keepdims=True)

        spot = lax.broadcasted_iota(jnp.int32, (8, 128), 1) == sub

        def along(column):
            return jnp.sum(jnp.where(spot, column, 0.0), axis=0, keepdims=True)[:, 0:8]

        for u in range(2):
            val = []
            for one, two in ((first, first), (second, second), (first, second), (second, first)):
                val.append([pick(tab[u, c], one, two) for c in range(2)])
            (ar, ai), (br, bi), (cr, ci), (dr, di) = val
            box = (
                (ar * br - ai * bi) - (cr * dr - ci * di),
                (ar * bi + ai * br) - (cr * di + ci * dr),
            )
            for c in range(2):
                cross = jnp.sum(jnp.sum(cacc[u, c], axis=1), axis=1, keepdims=True)
                box_ref[c, u : u + 1, :] = along(box[c])
                cross_ref[c, u : u + 1, :] = along(cross)

    def all_of(sem, count):
        ref = abuf_r.at[pl.ds(0, count)]
        return pltpu.make_async_copy(ref, ref, sem)

    a_all = [all_of(a_recv.at[h], 30) for h in range(2)]
    a_out = [all_of(a_send.at[h], 30) for h in range(2)]
    b_all = [all_of(b_recv.at[h], 15) for h in range(2)]
    b_out = [all_of(b_send.at[h], 15) for h in range(2)]

    def choose(h):
        abuf[h][pl.ds(2 * k, 2)] = ebuf[:, s, h, chunk(k), :]
        a_all[h].wait()
        for n in range(8):
            bsel[h, n] = abuf[h][times[n]]
        for d in range(1, 8):
            b_msg(h, d, True).start()
            b_msg(h, d, False).start()
        b_msg(h, 0, True).start()
        fbuf[s, h, chunk(k), :] = bsel[h, s]

    def spread(h):
        b_all[h].wait()
        for j in (0, 1, 2, 3):
            c_msg(h, j).start()
        k_msg(h, 0).start()

    def c_got(h, j):
        c_msg(h, j).wait_recv()

    def chunks_out(h):
        for d in range(1, 16):
            a_msg(h, d).start()

    def prepare():
        in_copy(2).wait()
        for u in range(2):
            real = pbuf[u, 0].astype(BF)
            imaginary = pbuf[u, 1].astype(BF)
            pw[u, 0:N, 0:N] = real
            pw[u, 0:N, N : 2 * N] = imaginary
            pw[u, N : 2 * N, 0:N] = -imaginary
            pw[u, N : 2 * N, N : 2 * N] = real
            ph[u, 0:N, 0:N] = real.T
            ph[u, 0:N, N : 2 * N] = imaginary.T
            ph[u, N : 2 * N, 0:N] = (-imaginary).T
            ph[u, N : 2 * N, N : 2 * N] = real.T

    chunks_out(0)
    chunks_out(1)
    go(0, 1, 2)
    go(1, 1, 2)
    prepare()
    go(0, 13)
    got(0, 2)
    go(0, 6)
    got(0, 1)
    go(0, 5)
    got(1, 2)
    go(1, 6)
    choose(0)
    got(1, 1)
    go(1, 5)
    choose(1)
    go(1, 13)
    go(1, 0)
    go(1, 9, 10)
    go(0, 9, 10)
    spread(0)
    go(1, 21)
    go(0, 21)
    go(0, 0)
    go(0, 17, 18)
    go(1, 17, 18)
    got(1, 10)
    go(1, 12)
    go(1, 15)
    got(1, 9)
    go(1, 11)
    go(1, 14)
    spread(1)
    c_msg(0, 0).wait_recv()
    c_msg(0, 4).start()
    c_msg(0, 1).wait_recv()
    c_msg(0, 5).start()
    got(0, 10)
    go(0, 15)
    go(0, 12)
    got(1, 0)
    go(1, 3, 20)
    got(0, 9)
    go(0, 14)
    go(0, 11)
    c_msg(0, 3).wait_recv()
    k_msg(0, 2).start()
    c_msg(0, 2).wait_recv()
    k_msg(0, 1).start()
    got(1, 21)
    go(1, 4, 19)
    got(0, 17, 18)
    chain(0, s, s_left, s_right)
    c_msg(1, 0).wait_recv()
    c_msg(1, 4).start()
    c_msg(1, 1).wait_recv()
    c_msg(1, 5).start()
    got(0, 21)
    go(0, 4, 19)
    got(1, 17, 18)
    chain(1, s, s_left, s_right)
    got(1, 13, 5, 6, 11, 12)
    chain(1, s_par, s_opp)
    c_msg(0, 4).wait_recv()
    k_msg(0, 3).start()
    c_msg(0, 5).wait_recv()
    k_msg(0, 4).start()
    got(0, 0)
    go(0, 3, 20)
    c_msg(1, 2).wait_recv()
    k_msg(1, 1).start()
    c_msg(1, 3).wait_recv()
    k_msg(1, 2).start()
    go(1, 16)
    got(1, 3)
    go(1, 7)
    c_msg(1, 4).wait_recv()
    k_msg(1, 3).start()
    c_msg(1, 5).wait_recv()
    k_msg(1, 4).start()
    got(0, 13, 5, 6, 11, 12)
    chain(0, s_par, s_opp)
    go(0, 16)
    k_msg(0, 0).wait_recv()
    k_msg(0, 1).wait_recv()
    k_msg(0, 2).wait_recv()
    k_msg(0, 3).wait_recv()
    k_msg(0, 4).wait_recv()
    k_msg(1, 0).wait_recv()
    k_msg(1, 1).wait_recv()
    k_msg(1, 2).wait_recv()
    k_msg(1, 3).wait_recv()
    k_msg(1, 4).wait_recv()
    loops(1, s)
    loops(1, s_left)
    loops(1, s_right)
    loops(0, s)
    loops(0, s_left)
    loops(0, s_right)
    got(1, 4)
    go(1, 8)
    got(1, 19, 14, 20, 15)
    chain(1, other(s_left), other(s_right))
    got(0, 4)
    go(0, 8)
    loops(0, s_par)
    loops(0, s_opp)
    got(0, 3)
    go(0, 7)
    loops(1, s_par)
    loops(1, s_opp)
    got(0, 19, 14, 20, 15)
    chain(0, other(s_left), other(s_right))
    loops(0, other(s_left))
    loops(0, other(s_right))
    got(1, 7, 8, 16)
    chain(1, other(s_opp))
    loops(1, other(s_opp))
    loops(1, other(s_left))
    loops(1, other(s_right))
    got(0, 7, 8, 16)
    chain(0, other(s_opp))
    trace_table(0)
    loops(0, other(s_opp))
    crossed(0, 0)
    crossed(0, 1)
    crossed(0, 2)
    crossed(0, 3)
    crossed(0, 4)
    crossed(0, 5)
    crossed(0, 6)
    crossed(0, 7)
    trace_table(1)
    crossed(1, 0)
    crossed(1, 1)
    crossed(1, 2)
    crossed(1, 3)
    crossed(1, 4)
    crossed(1, 5)
    crossed(1, 6)
    crossed(1, 7)
    finish()

    for h in range(2):
        a_out[h].wait()
        b_out[h].wait()
    for t in range(2):
        for j in range(22):
            e_msg(t, j).wait_send()
    for h in range(2):
        for j in range(6):
            c_msg(h, j).wait_send()
        for j in range(5):
            k_msg(h, j).wait_send()


def local(elementals, perambulators, source_times, pair_index):
    vm = pl.BlockSpec(memory_space=pltpu.VMEM)
    sm = pl.BlockSpec(memory_space=pltpu.SMEM)
    hbm = pl.BlockSpec(memory_space=pl.ANY)
    dma = pltpu.SemaphoreType.DMA
    boxes, crossed = pl.pallas_call(
        kernel,
        out_shape=(
            jax.ShapeDtypeStruct((2, 2, 8), F32),
            jax.ShapeDtypeStruct((2, 2, 8), F32),
        ),
        in_specs=[sm, sm, hbm, hbm],
        out_specs=(vm, vm),
        scratch_shapes=[
            pltpu.VMEM((2, 8, 2, N, N), BF),
            pltpu.VMEM((2, 2, N, N), F32),
            pltpu.VMEM((32, 16, N), BF),
            pltpu.VMEM((32, 16, N), BF),
            pltpu.VMEM((2, 8, 16, N), BF),
            pltpu.VMEM((8, 2, N, N), BF),
            pltpu.VMEM((2, 2 * N, 2 * N), BF),
            pltpu.VMEM((2, 2 * N, 2 * N), BF),
            pltpu.VMEM((2, 8, 3, N, N), BF),
            pltpu.VMEM((2, 8, 2, N, N), BF),
            pltpu.VMEM((2, 8, 2, N, N), BF),
            pltpu.VMEM((2, 8, 2, N, N), BF),
            pltpu.VMEM((2, 8, 2, N, N), BF),
            pltpu.VMEM((2, 2, 8, 8, 128), F32),
            pltpu.VMEM((2, 2, 8, 128), F32),
            dma((3,)),
            dma((2, 22)),
            dma((2, 22)),
            dma((2,)),
            dma((2,)),
            dma((2,)),
            dma((2,)),
            dma((2, 6)),
            dma((2, 6)),
            dma((2, 5)),
            dma((2, 5)),
        ],
        compiler_params=pltpu.CompilerParams(
            collective_id=0, has_side_effects=True, vmem_limit_bytes=56 * 1024 * 1024
        ),
        name="diagrams",
    )(source_times, pair_index.T, elementals, perambulators)
    return tuple(v.transpose(0, 2, 1)[:, :, None, :] for v in (boxes, crossed))


def solution(mesh):
    return jax.shard_map(
        local,
        mesh=mesh,
        in_specs=(P("snk", "src", None, None, None), P("src", "snk", None, None, None), P(), P()),
        out_specs=(P(None, None, "src", "snk"), P(None, None, "src", "snk")),
        check_vma=False,
    )
```

```python
import functools

import jax
import jax.numpy as jnp
from jax import lax
from jax.experimental import pallas as pl
from jax.experimental.pallas import tpu as pltpu
from jax.sharding import PartitionSpec as P

BF = jnp.bfloat16
F32 = jnp.float32
MESH = pl.DeviceIdType.MESH
N = 256
G = 80
GM, HM = 32, 176
NN = (((1,), (0,)), ((), ()))
NT = (((1,), (1,)), ((), ()))
TN = (((0,), (0,)), ((), ()))


def mm(form, a, b):
    return lax.dot_general(a, b, form, preferred_element_type=F32)


def kernel(
    times,
    pairs,
    e_in,
    p_in,
    out_ref,
    ebuf,
    pbuf,
    abuf_r,
    abuf_i,
    bsel,
    fbuf,
    pw,
    ph,
    vb,
    lb,
    lt,
    mb,
    mt,
    cacc,
    tab,
    in_sem,
    e_send,
    e_recv,
    a_send,
    a_recv,
    b_send,
    b_recv,
    c_send,
    c_recv,
    k_send,
    k_recv,
):
    abuf = (abuf_r, abuf_i)
    s = lax.axis_index("src")
    k = lax.axis_index("snk")
    x, yl = s // 2, s % 2
    z, yh, core = k // 4, (k // 2) % 2, k % 2
    s_par = x * 2 + (1 - yl)
    s_right = ((x + 1) % 4) * 2 + yl
    s_left = ((x + 3) % 4) * 2 + yl
    s_opp = ((x + 2) % 4) * 2 + yl

    def other(m):
        return (m // 2) * 2 + (1 - m % 2)

    right, left, ypar = (s_right, k), (s_left, k), (s_par, k)

    khp = (z * 2 + (1 - yh)) * 2 + core

    barrier = pltpu.get_barrier_semaphore()
    for d in range(1, 16):
        pl.semaphore_signal(barrier, 1, device_id=(s, (k + d) % 16), device_id_type=MESH)
    for d in range(1, 8):
        for q in (k, khp):
            pl.semaphore_signal(barrier, 1, device_id=((s + d) % 8, q), device_id_type=MESH)

    def in_copy(n):
        if n < 2:
            return pltpu.make_async_copy(e_in.at[n, 0], ebuf.at[n, s], in_sem.at[n])
        return pltpu.make_async_copy(p_in.at[0], pbuf, in_sem.at[2])

    for n in range(3):
        in_copy(n).start()
    in_copy(0).wait()
    in_copy(1).wait()
    pl.semaphore_wait(barrier, 29)

    def rows(ref, lo, hi):
        return ref.at[:, pl.ds(lo, hi - lo), :]

    def e_msg(t, j):
        own = ebuf.at[t, s]
        table = [
            (own, s, G, HM, ypar),
            (own, s, G, HM, right),
            (own, s, HM, N, left),
            (None, s_par, G, HM, right),
            (None, s_par, HM, N, left),
            (None, s_left, G, HM, right),
            (None, s_right, HM, N, left),
            (None, other(s_left), G, HM, right),
            (None, other(s_right), HM, N, left),
            (own, s, 0, G, right),
            (own, s, 0, G, left),
            (None, s_left, 0, GM, right),
            (None, s_right, GM, G, left),
            (own, s, 0, G, ypar),
            (None, s_left, 0, G, ypar),
            (None, s_right, 0, G, ypar),
            (None, s_opp, 0, G, ypar),
            (own, s, HM, N, right),
            (own, s, G, HM, left),
            (None, s_par, HM, N, right),
            (None, s_par, G, HM, left),
            (own, s, HM, N, ypar),
        ]
        src, m, lo, hi, dev = table[j]
        dst = ebuf.at[t, m]
        src = dst if src is None else src
        return pltpu.make_async_remote_copy(
            rows(src, lo, hi),
            rows(dst, lo, hi),
            e_send.at[t, j],
            e_recv.at[t, j],
            device_id=dev,
            device_id_type=MESH,
        )

    def go(t, *js):
        for j in js:
            e_msg(t, j).start()

    def got(t, *js):
        for j in js:
            e_msg(t, j).wait_recv()

    def place_of(q):
        return (q % 2) * 8 + q // 2

    def chunk(q):
        return pl.ds(pl.multiple_of(place_of(q) * 16, 16), 16)

    def chunks(zz, cc):
        return pl.ds(pl.multiple_of(cc * 128 + zz * 32, 32), 32)

    def a_msg(h, d):
        q = (k + d) % 16
        return pltpu.make_async_remote_copy(
            ebuf.at[:, s, h, chunk(q), :],
            abuf[h].at[pl.ds(2 * k, 2)],
            a_send.at[h],
            a_recv.at[h],
            device_id=(s, q),
            device_id_type=MESH,
        )

    def b_msg(h, d, far):
        q = (s + d) % 8
        return pltpu.make_async_remote_copy(
            bsel.at[h, q],
            fbuf.at[s, h, chunk(k), :],
            b_send.at[h],
            b_recv.at[h],
            device_id=(q, khp if far else k),
            device_id_type=MESH,
        )

    zr, zl, zo = (z + 1) % 4, (z + 3) % 4, (z + 2) % 4
    to_zr, to_zl = (s, (zr * 2 + yh) * 2 + core), (s, (zl * 2 + yh) * 2 + core)
    to_core = (s, (z * 2 + yh) * 2 + 1 - core)

    def c_msg(h, j):
        zz, lo, dev = [
            (z, 0, to_zr),
            (z, 4, to_zl),
            (z, 4, to_zr),
            (z, 0, to_zl),
            (zl, 0, to_zr),
            (zr, 4, to_zl),
        ][j]
        ref = fbuf.at[pl.ds(lo, 4), h, chunks(zz, core), :]
        return pltpu.make_async_remote_copy(
            ref, ref, c_send.at[h, j], c_recv.at[h, j], device_id=dev, device_id_type=MESH
        )

    def k_msg(h, j):
        zz, lo, count = [(z, 0, 8), (zl, 0, 8), (zr, 0, 8), (zo, 0, 4), (zo, 4, 4)][j]
        ref = fbuf.at[pl.ds(lo, count), h, chunks(zz, core), :]
        return pltpu.make_async_remote_copy(
            ref, ref, k_send.at[h, j], k_recv.at[h, j], device_id=to_core, device_id_type=MESH
        )

    def chain(u, *ms):
        lhs = jnp.concatenate(
            [jnp.concatenate([ebuf[u, m, 0], ebuf[u, m, 1]], axis=1) for m in ms], axis=0
        )
        out = mm(NN, lhs, pw[u]).astype(BF)
        rhs = [
            jnp.concatenate([out[i * N : (i + 1) * N, c * N : (c + 1) * N] for c in range(2)], axis=0)
            for i in range(len(ms))
        ]
        out = mm(NN, ph[u], jnp.concatenate(rhs, axis=1)).astype(BF)
        for i, m in enumerate(ms):
            real, imaginary = (out[c * N : (c + 1) * N, i * N : (i + 1) * N] for c in range(2))
            vb[u, m, 0] = real
            vb[u, m, 1] = imaginary
            vb[u, m, 2] = -real

    def loops(u, m):
        vr, vi, vn = vb[u, m, 0], vb[u, m, 1], vb[u, m, 2]
        fr, fi = fbuf[m, 0], fbuf[m, 1]
        f_row = jnp.concatenate([fr, fi], axis=1)
        f_col = jnp.concatenate([fr, fi], axis=0)
        for c, (one, two) in enumerate(((vr, vi), (vi, vn))):
            out = mm(NT, jnp.concatenate([one, two], axis=1), f_row).astype(BF)
            lb[u, m, c] = out
            lt[u, m, c] = out.T
        for c, (one, two) in enumerate(((vr, vi), (vi, vn))):
            out = mm(TN, f_col, jnp.concatenate([one, two], axis=0)).astype(BF)
            mb[u, m, c] = out
            mt[u, m, c] = out.T

    def crossed(u, n):
        a, b = pairs[0, n], pairs[1, n]
        re = jnp.zeros((16, N), F32)
        im = jnp.zeros((16, N), F32)
        for i in range(16):
            r = pl.ds(i * 16, 16)
            for one, two, sign in ((lb, lt, 1.0), (mb, mt, -1.0)):
                ar, ai = one[u, a, 0, r, :].astype(F32), one[u, a, 1, r, :].astype(F32)
                br, bi = two[u, b, 0, r, :].astype(F32), two[u, b, 1, r, :].astype(F32)
                if sign > 0:
                    re = re + (ar * br - ai * bi)
                    im = im + (ar * bi + ai * br)
                else:
                    re = re - (ar * br - ai * bi)
                    im = im - (ar * bi + ai * br)
        for c, v in enumerate((re, im)):
            v = v[0:8] + v[8:16]
            cacc[u, c, n] = v[:, 0:128] + v[:, 128:256]

    def trace_table(u):
        def side(ref, i):
            r = pl.ds(i * 16, 16)
            return jnp.concatenate([ref[:, c, r, :].reshape(128, N) for c in range(2)], axis=0)

        total = mm(
            NT,
            jnp.concatenate([side(vb.at[u], i) for i in range(16)], axis=1),
            jnp.concatenate([side(fbuf, i) for i in range(16)], axis=1),
        )
        real = total[0:128, 0:128] + total[128:256, 128:256]
        imaginary = total[128:256, 0:128] - total[0:128, 128:256]
        row = lax.broadcasted_iota(jnp.int32, (128, 128), 0) % 16
        col = lax.broadcasted_iota(jnp.int32, (128, 128), 1) % 16
        for c, part in enumerate((real, imaginary)):
            part = jnp.where(row == col, part, 0.0)
            tab[u, c] = jnp.sum(part.reshape(8, 16, 128), axis=1)

    def finish(u):
        sub = lax.broadcasted_iota(jnp.int32, (8, 128), 0)
        lane = lax.broadcasted_iota(jnp.int32, (8, 128), 1) // 16
        first = jnp.zeros((8, 128), jnp.int32)
        second = jnp.zeros((8, 128), jnp.int32)
        for n in range(8):
            first = jnp.where(sub == n, pairs[0, n], first)
            second = jnp.where(sub == n, pairs[1, n], second)

        def pick(table, one, two):
            got_rows = jnp.zeros((8, 128), F32)
            for m in range(8):
                got_rows = got_rows + jnp.where(one == m, table[m : m + 1, :], 0.0)
            return jnp.sum(jnp.where(lane == two, got_rows, 0.0), axis=1, keepdims=True)

        spot = lax.broadcasted_iota(jnp.int32, (8, 128), 1) == sub

        def along(column):
            return jnp.sum(jnp.where(spot, column, 0.0), axis=0, keepdims=True)[:, 0:8]

        val = []
        for one, two in ((first, first), (second, second), (first, second), (second, first)):
            val.append([pick(tab[u, c], one, two) for c in range(2)])
        (ar, ai), (br, bi), (cr, ci), (dr, di) = val
        box = (
            (ar * br - ai * bi) - (cr * dr - ci * di),
            (ar * bi + ai * br) - (cr * di + ci * dr),
        )
        for c in range(2):
            cross = jnp.sum(jnp.sum(cacc[u, c], axis=1), axis=1, keepdims=True)
            out_ref[0, c, u : u + 1, :] = along(box[c])
            out_ref[1, c, u : u + 1, :] = along(cross)

    def all_of(sem, count):
        ref = abuf_r.at[pl.ds(0, count)]
        return pltpu.make_async_copy(ref, ref, sem)

    a_all = [all_of(a_recv.at[h], 30) for h in range(2)]
    a_out = [all_of(a_send.at[h], 30) for h in range(2)]
    b_all = [all_of(b_recv.at[h], 15) for h in range(2)]
    b_out = [all_of(b_send.at[h], 15) for h in range(2)]

    def choose(h):
        abuf[h][pl.ds(2 * k, 2)] = ebuf[:, s, h, chunk(k), :]
        a_all[h].wait()
        for n in range(8):
            bsel[h, n] = abuf[h][times[n]]
        for d in range(1, 8):
            b_msg(h, d, True).start()
            b_msg(h, d, False).start()
        b_msg(h, 0, True).start()
        fbuf[s, h, chunk(k), :] = bsel[h, s]

    def spread(h):
        b_all[h].wait()
        for j in (0, 1, 2, 3):
            c_msg(h, j).start()
        k_msg(h, 0).start()

    def c_got(h, j):
        c_msg(h, j).wait_recv()

    def chunks_out(h):
        for d in range(1, 16):
            a_msg(h, d).start()

    def prepare():
        in_copy(2).wait()
        for u in range(2):
            real = pbuf[u, 0].astype(BF)
            imaginary = pbuf[u, 1].astype(BF)
            pw[u, 0:N, 0:N] = real
            pw[u, 0:N, N : 2 * N] = imaginary
            pw[u, N : 2 * N, 0:N] = -imaginary
            pw[u, N : 2 * N, N : 2 * N] = real
            ph[u, 0:N, 0:N] = real.T
            ph[u, 0:N, N : 2 * N] = imaginary.T
            ph[u, N : 2 * N, 0:N] = (-imaginary).T
            ph[u, N : 2 * N, N : 2 * N] = real.T

    chunks_out(0)
    chunks_out(1)
    go(1, 1, 2)
    go(0, 17, 18)
    prepare()
    go(1, 13)
    go(1, 17, 18)
    got(1, 2)
    go(1, 6)
    got(1, 1)
    go(1, 5)
    choose(0)
    choose(1)
    go(0, 1, 2)
    go(0, 9, 10)
    go(0, 13)
    go(0, 0)
    spread(0)
    go(0, 21)
    go(1, 0)
    go(1, 9, 10)
    got(0, 2)
    go(0, 6)
    got(0, 1)
    go(0, 5)
    spread(1)
    go(1, 21)
    got(0, 10)
    go(0, 15)
    go(0, 12)
    got(0, 9)
    go(0, 14)
    got(0, 0)
    go(0, 3, 20)
    go(0, 11)
    got(0, 17, 18)
    chain(0, s, s_left, s_right)
    c_msg(0, 0).wait_recv()
    c_msg(0, 4).start()
    got(1, 10)
    go(1, 15)
    c_msg(0, 1).wait_recv()
    c_msg(0, 5).start()
    go(1, 12)
    got(1, 9)
    go(1, 11)
    got(0, 21)
    go(0, 4, 19)
    c_msg(0, 3).wait_recv()
    k_msg(0, 2).start()
    got(1, 17, 18)
    chain(1, s, s_left, s_right)
    go(1, 14)
    c_msg(0, 2).wait_recv()
    k_msg(0, 1).start()
    c_msg(1, 1).wait_recv()
    c_msg(1, 5).start()
    c_msg(1, 0).wait_recv()
    c_msg(1, 4).start()
    got(1, 0)
    go(1, 3, 20)
    c_msg(1, 2).wait_recv()
    k_msg(1, 1).start()
    c_msg(1, 3).wait_recv()
    k_msg(1, 2).start()
    got(1, 21)
    go(1, 4, 19)
    got(0, 3)
    go(0, 7)
    c_msg(0, 4).wait_recv()
    k_msg(0, 3).start()
    c_msg(0, 5).wait_recv()
    k_msg(0, 4).start()
    got(0, 13, 5, 6, 11, 12)
    chain(0, s_par, s_opp)
    c_msg(1, 5).wait_recv()
    k_msg(1, 4).start()
    c_msg(1, 4).wait_recv()
    k_msg(1, 3).start()
    got(1, 13, 5, 6, 11, 12)
    chain(1, s_par, s_opp)
    go(1, 16)
    go(0, 16)
    got(0, 4)
    go(0, 8)
    got(0, 19, 14, 20, 15)
    chain(0, other(s_left), other(s_right))
    k_msg(0, 0).wait_recv()
    k_msg(0, 1).wait_recv()
    k_msg(0, 2).wait_recv()
    k_msg(0, 3).wait_recv()
    k_msg(0, 4).wait_recv()
    k_msg(1, 0).wait_recv()
    k_msg(1, 1).wait_recv()
    k_msg(1, 2).wait_recv()
    k_msg(1, 3).wait_recv()
    k_msg(1, 4).wait_recv()
    loops(1, s)
    loops(1, s_left)
    loops(1, s_right)
    loops(0, s)
    loops(0, s_left)
    loops(0, s_right)
    loops(0, other(s_left))
    loops(0, other(s_right))
    got(1, 3, 19, 14, 4, 20, 15)
    chain(1, other(s_left), other(s_right))
    go(1, 7)
    go(1, 8)
    loops(0, s_par)
    loops(0, s_opp)
    loops(1, s_par)
    loops(1, s_opp)
    loops(1, other(s_left))
    loops(1, other(s_right))
    got(0, 7, 8, 16)
    chain(0, other(s_opp))
    trace_table(0)
    loops(0, other(s_opp))
    crossed(0, 0)
    crossed(0, 1)
    crossed(0, 2)
    crossed(0, 3)
    crossed(0, 4)
    crossed(0, 5)
    crossed(0, 6)
    crossed(0, 7)
    finish(0)
    got(1, 7, 8, 16)
    chain(1, other(s_opp))
    loops(1, other(s_opp))
    trace_table(1)
    crossed(1, 0)
    crossed(1, 1)
    crossed(1, 2)
    crossed(1, 3)
    crossed(1, 4)
    crossed(1, 5)
    crossed(1, 6)
    crossed(1, 7)
    finish(1)

    for h in range(2):
        a_out[h].wait()
        b_out[h].wait()
    for t in range(2):
        for j in range(22):
            e_msg(t, j).wait_send()
    for h in range(2):
        for j in range(6):
            c_msg(h, j).wait_send()
        for j in range(5):
            k_msg(h, j).wait_send()


def local(elementals, perambulators, source_times, pair_index):
    vm = pl.BlockSpec(memory_space=pltpu.VMEM)
    sm = pl.BlockSpec(memory_space=pltpu.SMEM)
    hbm = pl.BlockSpec(memory_space=pl.ANY)
    dma = pltpu.SemaphoreType.DMA
    both = pl.pallas_call(
        kernel,
        out_shape=jax.ShapeDtypeStruct((2, 2, 2, 8), F32),
        in_specs=[sm, sm, hbm, hbm],
        out_specs=vm,
        scratch_shapes=[
            pltpu.VMEM((2, 8, 2, N, N), BF),
            pltpu.VMEM((2, 2, N, N), F32),
            pltpu.VMEM((32, 16, N), BF),
            pltpu.VMEM((32, 16, N), BF),
            pltpu.VMEM((2, 8, 16, N), BF),
            pltpu.VMEM((8, 2, N, N), BF),
            pltpu.VMEM((2, 2 * N, 2 * N), BF),
            pltpu.VMEM((2, 2 * N, 2 * N), BF),
            pltpu.VMEM((2, 8, 3, N, N), BF),
            pltpu.VMEM((2, 8, 2, N, N), BF),
            pltpu.VMEM((2, 8, 2, N, N), BF),
            pltpu.VMEM((2, 8, 2, N, N), BF),
            pltpu.VMEM((2, 8, 2, N, N), BF),
            pltpu.VMEM((2, 2, 8, 8, 128), F32),
            pltpu.VMEM((2, 2, 8, 128), F32),
            dma((3,)),
            dma((2, 22)),
            dma((2, 22)),
            dma((2,)),
            dma((2,)),
            dma((2,)),
            dma((2,)),
            dma((2, 6)),
            dma((2, 6)),
            dma((2, 5)),
            dma((2, 5)),
        ],
        compiler_params=pltpu.CompilerParams(
            collective_id=0, has_side_effects=True, vmem_limit_bytes=56 * 1024 * 1024
        ),
        name="diagrams",
    )(source_times, pair_index.T, elementals, perambulators)
    return tuple(v.transpose(0, 2, 1)[:, :, None, :] for v in (both[0], both[1]))


def solution(mesh):
    return jax.shard_map(
        local,
        mesh=mesh,
        in_specs=(P("snk", "src", None, None, None), P("src", "snk", None, None, None), P(), P()),
        out_specs=(P(None, None, "src", "snk"), P(None, None, "src", "snk")),
        check_vma=False,
    )
```

```python
import functools

import jax
import jax.numpy as jnp
from jax import lax
from jax.experimental import pallas as pl
from jax.experimental.pallas import tpu as pltpu
from jax.sharding import PartitionSpec as P

BF = jnp.bfloat16
F32 = jnp.float32
MESH = pl.DeviceIdType.MESH
N = 256
G = 80
GM, HM = 32, 176
NN = (((1,), (0,)), ((), ()))
NT = (((1,), (1,)), ((), ()))
TN = (((0,), (0,)), ((), ()))


def mm(form, a, b):
    return lax.dot_general(a, b, form, preferred_element_type=F32)


def kernel(
    times,
    pairs,
    e_in,
    p_in,
    out_ref,
    ebuf,
    pbuf,
    abuf_r,
    abuf_i,
    bsel,
    fbuf,
    pw,
    ph,
    vb,
    lb,
    lt,
    mb,
    mt,
    cacc,
    tab,
    in_sem,
    e_send,
    e_recv,
    a_send,
    a_recv,
    b_send,
    b_recv,
    c_send,
    c_recv,
    k_send,
    k_recv,
):
    abuf = (abuf_r, abuf_i)
    s = lax.axis_index("src")
    k = lax.axis_index("snk")
    x, yl = s // 2, s % 2
    z, yh, core = k // 4, (k // 2) % 2, k % 2
    s_par = x * 2 + (1 - yl)
    s_right = ((x + 1) % 4) * 2 + yl
    s_left = ((x + 3) % 4) * 2 + yl
    s_opp = ((x + 2) % 4) * 2 + yl

    def other(m):
        return (m // 2) * 2 + (1 - m % 2)

    right, left, ypar = (s_right, k), (s_left, k), (s_par, k)

    khp = (z * 2 + (1 - yh)) * 2 + core

    barrier = pltpu.get_barrier_semaphore()
    for d in range(1, 16):
        pl.semaphore_signal(barrier, 1, device_id=(s, (k + d) % 16), device_id_type=MESH)
    for d in range(1, 8):
        for q in (k, khp):
            pl.semaphore_signal(barrier, 1, device_id=((s + d) % 8, q), device_id_type=MESH)

    def in_copy(n):
        if n < 2:
            return pltpu.make_async_copy(e_in.at[n, 0], ebuf.at[n, s], in_sem.at[n])
        return pltpu.make_async_copy(p_in.at[0], pbuf, in_sem.at[2])

    for n in range(3):
        in_copy(n).start()
    in_copy(0).wait()
    in_copy(1).wait()
    pl.semaphore_wait(barrier, 29)

    def rows(ref, lo, hi):
        return ref.at[:, pl.ds(lo, hi - lo), :]

    def e_msg(t, j):
        own = ebuf.at[t, s]
        table = [
            (own, s, G, HM, ypar),
            (own, s, G, HM, right),
            (own, s, HM, N, left),
            (None, s_par, G, HM, right),
            (None, s_par, HM, N, left),
            (None, s_left, G, HM, right),
            (None, s_right, HM, N, left),
            (None, other(s_left), G, HM, right),
            (None, other(s_right), HM, N, left),
            (own, s, 0, G, right),
            (own, s, 0, G, left),
            (None, s_left, 0, GM, right),
            (None, s_right, GM, G, left),
            (own, s, 0, G, ypar),
            (None, s_left, 0, G, ypar),
            (None, s_right, 0, G, ypar),
            (None, s_opp, 0, G, ypar),
            (own, s, HM, N, right),
            (own, s, G, HM, left),
            (None, s_par, HM, N, right),
            (None, s_par, G, HM, left),
            (own, s, HM, N, ypar),
        ]
        src, m, lo, hi, dev = table[j]
        dst = ebuf.at[t, m]
        src = dst if src is None else src
        return pltpu.make_async_remote_copy(
            rows(src, lo, hi),
            rows(dst, lo, hi),
            e_send.at[t, j],
            e_recv.at[t, j],
            device_id=dev,
            device_id_type=MESH,
        )

    def go(t, *js):
        for j in js:
            e_msg(t, j).start()

    def got(t, *js):
        for j in js:
            e_msg(t, j).wait_recv()

    def place_of(q):
        return (q % 2) * 8 + q // 2

    def chunk(q):
        return pl.ds(pl.multiple_of(place_of(q) * 16, 16), 16)

    def chunks(zz, cc):
        return pl.ds(pl.multiple_of(cc * 128 + zz * 32, 32), 32)

    def a_msg(h, d):
        q = (k + d) % 16
        return pltpu.make_async_remote_copy(
            ebuf.at[:, s, h, chunk(q), :],
            abuf[h].at[pl.ds(2 * k, 2)],
            a_send.at[h],
            a_recv.at[h],
            device_id=(s, q),
            device_id_type=MESH,
        )

    def b_msg(h, d, far):
        q = (s + d) % 8
        return pltpu.make_async_remote_copy(
            bsel.at[h, q],
            fbuf.at[s, h, chunk(k), :],
            b_send.at[h],
            b_recv.at[h],
            device_id=(q, khp if far else k),
            device_id_type=MESH,
        )

    zr, zl, zo = (z + 1) % 4, (z + 3) % 4, (z + 2) % 4
    to_zr, to_zl = (s, (zr * 2 + yh) * 2 + core), (s, (zl * 2 + yh) * 2 + core)
    to_core = (s, (z * 2 + yh) * 2 + 1 - core)

    def c_msg(h, j):
        zz, lo, dev = [
            (z, 0, to_zr),
            (z, 4, to_zl),
            (z, 4, to_zr),
            (z, 0, to_zl),
            (zl, 0, to_zr),
            (zr, 4, to_zl),
        ][j]
        ref = fbuf.at[pl.ds(lo, 4), h, chunks(zz, core), :]
        return pltpu.make_async_remote_copy(
            ref, ref, c_send.at[h, j], c_recv.at[h, j], device_id=dev, device_id_type=MESH
        )

    def k_msg(h, j):
        zz, lo, count = [(z, 0, 8), (zl, 0, 8), (zr, 0, 8), (zo, 0, 4), (zo, 4, 4)][j]
        ref = fbuf.at[pl.ds(lo, count), h, chunks(zz, core), :]
        return pltpu.make_async_remote_copy(
            ref, ref, k_send.at[h, j], k_recv.at[h, j], device_id=to_core, device_id_type=MESH
        )

    def chain(u, *ms):
        lhs = jnp.concatenate(
            [jnp.concatenate([ebuf[u, m, 0], ebuf[u, m, 1]], axis=1) for m in ms], axis=0
        )
        out = mm(NN, lhs, pw[u]).astype(BF)
        rhs = [
            jnp.concatenate([out[i * N : (i + 1) * N, c * N : (c + 1) * N] for c in range(2)], axis=0)
            for i in range(len(ms))
        ]
        out = mm(NN, ph[u], jnp.concatenate(rhs, axis=1)).astype(BF)
        for i, m in enumerate(ms):
            real, imaginary = (out[c * N : (c + 1) * N, i * N : (i + 1) * N] for c in range(2))
            vb[u, m, 0] = real
            vb[u, m, 1] = imaginary
            vb[u, m, 2] = -real

    def loops(u, m):
        vr, vi, vn = vb[u, m, 0], vb[u, m, 1], vb[u, m, 2]
        fr, fi = fbuf[m, 0], fbuf[m, 1]
        f_row = jnp.concatenate([fr, fi], axis=1)
        f_col = jnp.concatenate([fr, fi], axis=0)
        for c, (one, two) in enumerate(((vr, vi), (vi, vn))):
            out = mm(NT, jnp.concatenate([one, two], axis=1), f_row).astype(BF)
            lb[u, m, c] = out
            lt[u, m, c] = out.T
        for c, (one, two) in enumerate(((vr, vi), (vi, vn))):
            out = mm(TN, f_col, jnp.concatenate([one, two], axis=0)).astype(BF)
            mb[u, m, c] = out
            mt[u, m, c] = out.T

    def crossed(u, n):
        a, b = pairs[0, n], pairs[1, n]
        re = jnp.zeros((16, N), F32)
        im = jnp.zeros((16, N), F32)
        for i in range(16):
            r = pl.ds(i * 16, 16)
            for one, two, sign in ((lb, lt, 1.0), (mb, mt, -1.0)):
                ar, ai = one[u, a, 0, r, :].astype(F32), one[u, a, 1, r, :].astype(F32)
                br, bi = two[u, b, 0, r, :].astype(F32), two[u, b, 1, r, :].astype(F32)
                if sign > 0:
                    re = re + (ar * br - ai * bi)
                    im = im + (ar * bi + ai * br)
                else:
                    re = re - (ar * br - ai * bi)
                    im = im - (ar * bi + ai * br)
        for c, v in enumerate((re, im)):
            v = v[0:8] + v[8:16]
            cacc[u, c, n] = v[:, 0:128] + v[:, 128:256]

    def trace_table(u):
        def side(ref, i):
            r = pl.ds(i * 16, 16)
            return jnp.concatenate([ref[:, c, r, :].reshape(128, N) for c in range(2)], axis=0)

        total = mm(
            NT,
            jnp.concatenate([side(vb.at[u], i) for i in range(16)], axis=1),
            jnp.concatenate([side(fbuf, i) for i in range(16)], axis=1),
        )
        real = total[0:128, 0:128] + total[128:256, 128:256]
        imaginary = total[128:256, 0:128] - total[0:128, 128:256]
        row = lax.broadcasted_iota(jnp.int32, (128, 128), 0) % 16
        col = lax.broadcasted_iota(jnp.int32, (128, 128), 1) % 16
        for c, part in enumerate((real, imaginary)):
            part = jnp.where(row == col, part, 0.0)
            tab[u, c] = jnp.sum(part.reshape(8, 16, 128), axis=1)

    def finish(u):
        sub = lax.broadcasted_iota(jnp.int32, (8, 128), 0)
        lane = lax.broadcasted_iota(jnp.int32, (8, 128), 1) // 16
        first = jnp.zeros((8, 128), jnp.int32)
        second = jnp.zeros((8, 128), jnp.int32)
        for n in range(8):
            first = jnp.where(sub == n, pairs[0, n], first)
            second = jnp.where(sub == n, pairs[1, n], second)

        def pick(table, one, two):
            got_rows = jnp.zeros((8, 128), F32)
            for m in range(8):
                got_rows = got_rows + jnp.where(one == m, table[m : m + 1, :], 0.0)
            return jnp.sum(jnp.where(lane == two, got_rows, 0.0), axis=1, keepdims=True)

        spot = lax.broadcasted_iota(jnp.int32, (8, 128), 1) == sub

        def along(column):
            return jnp.sum(jnp.where(spot, column, 0.0), axis=0, keepdims=True)[:, 0:8]

        val = []
        for one, two in ((first, first), (second, second), (first, second), (second, first)):
            val.append([pick(tab[u, c], one, two) for c in range(2)])
        (ar, ai), (br, bi), (cr, ci), (dr, di) = val
        box = (
            (ar * br - ai * bi) - (cr * dr - ci * di),
            (ar * bi + ai * br) - (cr * di + ci * dr),
        )
        for c in range(2):
            cross = jnp.sum(jnp.sum(cacc[u, c], axis=1), axis=1, keepdims=True)
            out_ref[0, c, u : u + 1, :] = along(box[c])
            out_ref[1, c, u : u + 1, :] = along(cross)

    def all_of(sem, count):
        ref = abuf_r.at[pl.ds(0, count)]
        return pltpu.make_async_copy(ref, ref, sem)

    a_all = [all_of(a_recv.at[h], 30) for h in range(2)]
    a_out = [all_of(a_send.at[h], 30) for h in range(2)]
    b_all = [all_of(b_recv.at[h], 15) for h in range(2)]
    b_out = [all_of(b_send.at[h], 15) for h in range(2)]

    def choose(h):
        abuf[h][pl.ds(2 * k, 2)] = ebuf[:, s, h, chunk(k), :]
        a_all[h].wait()
        for n in range(8):
            bsel[h, n] = abuf[h][times[n]]
        for d in range(1, 8):
            b_msg(h, d, True).start()
            b_msg(h, d, False).start()
        b_msg(h, 0, True).start()
        fbuf[s, h, chunk(k), :] = bsel[h, s]

    def spread(h):
        b_all[h].wait()
        for j in (0, 1, 2, 3):
            c_msg(h, j).start()
        k_msg(h, 0).start()

    def c_got(h, j):
        c_msg(h, j).wait_recv()

    def chunks_out(h):
        for d in range(1, 16):
            a_msg(h, d).start()

    def prepare():
        in_copy(2).wait()
        for u in range(2):
            real = pbuf[u, 0].astype(BF)
            imaginary = pbuf[u, 1].astype(BF)
            pw[u, 0:N, 0:N] = real
            pw[u, 0:N, N : 2 * N] = imaginary
            pw[u, N : 2 * N, 0:N] = -imaginary
            pw[u, N : 2 * N, N : 2 * N] = real
            ph[u, 0:N, 0:N] = real.T
            ph[u, 0:N, N : 2 * N] = imaginary.T
            ph[u, N : 2 * N, 0:N] = (-imaginary).T
            ph[u, N : 2 * N, N : 2 * N] = real.T

    chunks_out(0)
    chunks_out(1)
    go(1, 1, 2)
    go(0, 17, 18)
    prepare()
    go(1, 13)
    go(1, 17, 18)
    got(1, 2)
    go(1, 6)
    got(1, 1)
    go(1, 5)
    choose(0)
    choose(1)
    go(0, 1, 2)
    go(0, 9, 10)
    go(0, 13)
    go(0, 0)
    spread(0)
    go(0, 21)
    go(1, 0)
    go(1, 9, 10)
    got(0, 2)
    go(0, 6)
    got(0, 1)
    go(0, 5)
    spread(1)
    go(1, 21)
    got(0, 10)
    go(0, 15)
    go(0, 12)
    got(0, 9)
    go(0, 14)
    got(0, 0)
    go(0, 3, 20)
    go(0, 11)
    got(0, 17, 18)
    chain(0, s, s_left, s_right)
    c_msg(0, 0).wait_recv()
    c_msg(0, 4).start()
    got(1, 10)
    go(1, 15)
    c_msg(0, 1).wait_recv()
    c_msg(0, 5).start()
    go(1, 12)
    got(1, 9)
    go(1, 11)
    got(0, 21)
    go(0, 4, 19)
    c_msg(0, 3).wait_recv()
    k_msg(0, 2).start()
    got(1, 17, 18)
    chain(1, s, s_left, s_right)
    go(1, 14)
    c_msg(0, 2).wait_recv()
    k_msg(0, 1).start()
    c_msg(1, 1).wait_recv()
    c_msg(1, 5).start()
    c_msg(1, 0).wait_recv()
    c_msg(1, 4).start()
    got(1, 0)
    go(1, 3, 20)
    c_msg(1, 2).wait_recv()
    k_msg(1, 1).start()
    c_msg(1, 3).wait_recv()
    k_msg(1, 2).start()
    got(1, 21)
    go(1, 4, 19)
    got(0, 3)
    go(0, 7)
    c_msg(0, 4).wait_recv()
    k_msg(0, 3).start()
    c_msg(0, 5).wait_recv()
    k_msg(0, 4).start()
    got(0, 13, 5, 6, 11, 12)
    chain(0, s_par, s_opp)
    c_msg(1, 5).wait_recv()
    k_msg(1, 4).start()
    c_msg(1, 4).wait_recv()
    k_msg(1, 3).start()
    got(1, 13, 5, 6, 11, 12)
    chain(1, s_par, s_opp)
    go(1, 16)
    go(0, 16)
    got(0, 4)
    go(0, 8)
    got(0, 19, 14, 20, 15)
    chain(0, other(s_left), other(s_right))
    k_msg(0, 0).wait_recv()
    k_msg(0, 1).wait_recv()
    k_msg(0, 2).wait_recv()
    k_msg(0, 3).wait_recv()
    k_msg(0, 4).wait_recv()
    k_msg(1, 0).wait_recv()
    k_msg(1, 1).wait_recv()
    k_msg(1, 2).wait_recv()
    k_msg(1, 3).wait_recv()
    k_msg(1, 4).wait_recv()
    loops(1, s)
    loops(1, s_left)
    loops(1, s_right)
    loops(0, s)
    loops(0, s_left)
    loops(0, s_right)
    loops(0, other(s_left))
    loops(0, other(s_right))
    got(1, 3, 4)
    go(1, 7, 8)
    got(1, 19, 14, 20, 15)
    chain(1, other(s_left), other(s_right))
    loops(0, s_par)
    loops(0, s_opp)
    loops(1, s_par)
    loops(1, s_opp)
    loops(1, other(s_left))
    loops(1, other(s_right))
    got(0, 7, 8, 16)
    chain(0, other(s_opp))
    trace_table(0)
    loops(0, other(s_opp))
    crossed(0, 0)
    crossed(0, 1)
    crossed(0, 2)
    crossed(0, 3)
    crossed(0, 4)
    crossed(0, 5)
    crossed(0, 6)
    crossed(0, 7)
    finish(0)
    for h in range(2):
        a_out[h].wait()
        b_out[h].wait()
        for j in range(6):
            c_msg(h, j).wait_send()
        for j in range(5):
            k_msg(h, j).wait_send()
    late = (7, 8, 16)
    for t in range(2):
        for j in range(22):
            if j not in late:
                e_msg(t, j).wait_send()
    got(1, 7, 8, 16)
    chain(1, other(s_opp))
    loops(1, other(s_opp))
    trace_table(1)
    crossed(1, 0)
    crossed(1, 1)
    crossed(1, 2)
    crossed(1, 3)
    crossed(1, 4)
    crossed(1, 5)
    crossed(1, 6)
    crossed(1, 7)
    finish(1)

    for t in range(2):
        for j in late:
            e_msg(t, j).wait_send()


def local(elementals, perambulators, source_times, pair_index):
    vm = pl.BlockSpec(memory_space=pltpu.VMEM)
    sm = pl.BlockSpec(memory_space=pltpu.SMEM)
    hbm = pl.BlockSpec(memory_space=pl.ANY)
    dma = pltpu.SemaphoreType.DMA
    both = pl.pallas_call(
        kernel,
        out_shape=jax.ShapeDtypeStruct((2, 2, 2, 8), F32),
        in_specs=[sm, sm, hbm, hbm],
        out_specs=vm,
        scratch_shapes=[
            pltpu.VMEM((2, 8, 2, N, N), BF),
            pltpu.VMEM((2, 2, N, N), F32),
            pltpu.VMEM((32, 16, N), BF),
            pltpu.VMEM((32, 16, N), BF),
            pltpu.VMEM((2, 8, 16, N), BF),
            pltpu.VMEM((8, 2, N, N), BF),
            pltpu.VMEM((2, 2 * N, 2 * N), BF),
            pltpu.VMEM((2, 2 * N, 2 * N), BF),
            pltpu.VMEM((2, 8, 3, N, N), BF),
            pltpu.VMEM((2, 8, 2, N, N), BF),
            pltpu.VMEM((2, 8, 2, N, N), BF),
            pltpu.VMEM((2, 8, 2, N, N), BF),
            pltpu.VMEM((2, 8, 2, N, N), BF),
            pltpu.VMEM((2, 2, 8, 8, 128), F32),
            pltpu.VMEM((2, 2, 8, 128), F32),
            dma((3,)),
            dma((2, 22)),
            dma((2, 22)),
            dma((2,)),
            dma((2,)),
            dma((2,)),
            dma((2,)),
            dma((2, 6)),
            dma((2, 6)),
            dma((2, 5)),
            dma((2, 5)),
        ],
        compiler_params=pltpu.CompilerParams(
            collective_id=0, has_side_effects=True, vmem_limit_bytes=56 * 1024 * 1024
        ),
        name="diagrams",
    )(source_times, pair_index.T, elementals, perambulators)
    return tuple(v.transpose(0, 2, 1)[:, :, None, :] for v in (both[0], both[1]))


def solution(mesh):
    return jax.shard_map(
        local,
        mesh=mesh,
        in_specs=(P("snk", "src", None, None, None), P("src", "snk", None, None, None), P(), P()),
        out_specs=(P(None, None, "src", "snk"), P(None, None, "src", "snk")),
        check_vma=False,
    )
```
